256 devices in a mesh: px: 16 (over x_lo, z), py: 16 (over y, x_hi, core).
Axes of the slice: x: 4 (x_hi: 2, x_lo: 2; x = x_hi * 2 + x_lo), y: 4, z: 8, core: 2. Of those that a mesh axis runs over, the one named last changes fastest.
Arguments:
- inputs: float32 [64, 256, 8192], P(None, 'px', 'py'), may hold values from -6 to 6
- pre_act: float32 [64, 256, 8192], P(None, 'px', 'py'), may hold values from -8 to 8
- cotangent: float32 [64, 256, 8192], P(None, 'px', 'py'), may hold values from -6 to 6
- mix_weight: float32 [64, 64], replicated, may hold values from -0.75 to 0.75
- spectral_weight: float32 [32, 32, 8, 64, 128], P('py', 'px'), may hold values from -6 to 6
Outputs:
- input_grad: float32 [64, 256, 8192], P(None, 'px', 'py')
- spectral_grad: float32 [32, 32, 8, 64, 128], P('py', 'px')
- mix_grad: float32 [64, 64], replicated
The draws below stay inside these ranges and needn't reach their ends.
All inputs are finite; a program needn't handle non-finite values.
Results may differ from the reference program's by a relative error of at most 0.0001.
Values sent between devices are 32-bit elements; how exact they have to be, the bound alone decides.
No kernel may reach another device: no remote copies, remote signals or barrier semaphores. Data moves between devices by JAX's collectives and lax.ppermute only.
A program may use at most 192 MiB of HBM per device.

```python
import math
import jax
import jax.numpy as jnp
from jax import lax

C = 64
NX = 256
NY = 256
NZ = 32
MX = 16
MY = 16
MZ = 8
KX = 32
KY = 32
CELLS = 2097152


def block_scale(key, shape, pieces, low, high):
    def one(dim, blocks):
        heights = jax.random.uniform(jax.random.fold_in(jax.random.fold_in(key, 6), dim), (blocks,), jnp.float32, low / len(pieces), high / len(pieces))
        return jnp.repeat(jnp.exp(heights), shape[dim] // blocks).reshape((-1,) + (1,) * (len(shape) - dim - 1))

    factor_of = one(*pieces[0])
    for cut in pieces[1:]:
        factor_of = factor_of * one(*cut)
    return factor_of


def bell_draw(rng, shape, deviation, reach, cuts=(), held_as=jnp.bfloat16):
    array = jax.random.normal(rng, shape, jnp.float32) * deviation
    if len(cuts) > 0:
        array = block_scale(rng, shape, cuts, -0.22, 0.18) * array
    return jnp.clip(array, min=-reach, max=reach).astype(held_as)


def setup_inputs(seed: int = 0) -> dict:
    keys = jax.random.split(jax.random.key(seed), 6)
    return {
        "inputs": bell_draw(keys[0], (C, NX, NY * NZ), 1.0, 6.0, ((1, 16), (2, 16)), jnp.float32),
        "pre_act": bell_draw(keys[1], (C, NX, NY * NZ), 1.5, 8.0, ((1, 16), (2, 16)), jnp.float32),
        "cotangent": bell_draw(keys[2], (C, NX, NY * NZ), 1.0, 6.0, ((1, 16), (2, 16)), jnp.float32),
        "mix_weight": bell_draw(keys[3], (C, C), C ** -0.5, 0.75, (), jnp.float32),
        "spectral_weight": bell_draw(keys[4], (KX, KY, MZ, C, 2 * C), 1.0, 6.0, ((0, 16), (1, 16)), jnp.float32),
    }


def product(pattern, first_operand, second_operand):
    return jnp.einsum(pattern, first_operand, second_operand, precision=lax.Precision.HIGHEST)

def gelu_slope(values):
    cumulative = 0.5 * (1.0 + jax.scipy.special.erf(values / math.sqrt(2.0)))
    density = jnp.exp(-0.5 * values * values) / math.sqrt(2.0 * math.pi)
    return cumulative + values * density

def retained(half_span, length):
    return jnp.concatenate([jnp.arange(half_span), length - half_span + jnp.arange(half_span)]).astype(jnp.int32)

def spectrum(field_data):
    shaped_grid = field_data.reshape(C, NX, NY, NZ)
    index_first = retained(MX, NX)
    index_second = retained(MY, NY)

    def one_channel(channel_grid):
        transform = jnp.fft.fftn(channel_grid)
        return transform[index_first][:, index_second][:, :, :MZ]
    return lax.map(one_channel, shaped_grid)

def reference(inputs, pre_act, cotangent, mix_weight, spectral_weight):
    grad_pre = cotangent * gelu_slope(pre_act)
    mix_grad = product('cxs,oxs->co', inputs, grad_pre) / math.sqrt(CELLS)
    input_spectrum = spectrum(inputs)
    weighting = jnp.where(jnp.arange(MZ) == 0, 1.0, 2.0) / CELLS
    output_spectrum = spectrum(grad_pre) * weighting
    weight_complex = lax.complex(spectral_weight[..., :C], spectral_weight[..., C:])
    outer_product = product('cpqk,opqk->pqkco', jnp.conj(input_spectrum), output_spectrum)
    spectral_grad = jnp.concatenate([jnp.real(outer_product), jnp.imag(outer_product)], axis=-1)
    mode_grad = product('pqkco,opqk->cpqk', jnp.conj(weight_complex), output_spectrum)
    index_first = retained(MX, NX)
    index_second = retained(MY, NY)
    index_depth = jnp.arange(MZ).astype(jnp.int32)

    def back_channel(channel_modes):
        padded = jnp.zeros((NX, NY, NZ), channel_modes.dtype)
        padded = padded.at[index_first[:, None, None], index_second[None, :, None], index_depth[None, None, :]].set(channel_modes)
        return jnp.real(jnp.fft.ifftn(padded)) * CELLS
    spatial = lax.map(back_channel, mode_grad).reshape(C, NX, NY * NZ)
    input_grad = product('co,oxs->cxs', mix_weight, grad_pre) + spatial
    return (input_grad, spectral_grad, mix_grad)
```

```python
import math

import jax
import jax.numpy as jnp
import ml_dtypes
import numpy as np
from jax import lax
from jax.experimental import pallas as pl
from jax.experimental.pallas import tpu as pltpu
from jax.sharding import PartitionSpec as P

C = 64
NX = 256
NY = 256
NZ = 32
MZ = 8
CELLS = NX * NY * NZ
N = 16
F32 = jnp.float32
BF16 = jnp.bfloat16


def pair(table):
    high = table.astype(ml_dtypes.bfloat16)
    low = (table - high.astype(np.float64)).astype(high.dtype)
    return high, low


def frequency(index):
    return np.where(index < 16, index, index - 32)


def angle(a, b, length):
    return 2.0 * np.pi / length * np.mod(a * b, length)


def depth_forward():
    k, z = np.arange(8)[:, None], np.arange(32)[None, :]
    t = angle(k, z, 32)
    parts = np.stack([np.cos(t), -np.sin(t)], 1)
    return np.einsum("krz,ab->krabz", parts, np.eye(16)).reshape(256, 512)


def depth_inverse():
    return depth_forward().reshape(4, 2, 2, 16, 512).transpose(1, 0, 2, 3, 4).reshape(256, 512)


def second_forward():
    q = np.arange(32)
    t = angle(frequency(q)[:, None], np.arange(256)[None, :], 256)
    c, s = np.cos(t), np.sin(t)
    full = np.stack([np.stack([c, s], 1), np.stack([-s, c], 1)], 0)
    full = full.reshape(2, 16, 2, 2, 16, 16)
    return full.transpose(0, 2, 1, 4, 3, 5).reshape(64, 512)


def second_inverse():
    q = np.arange(32)
    t = angle(frequency(q)[:, None], np.arange(256)[None, :], 256)
    c, s = np.cos(t), np.sin(t)
    full = np.stack([np.stack([c, s], 0), np.stack([-s, c], 0)], 0)
    full = full.reshape(2, 2, 16, 2, 16, 16)
    return full.transpose(4, 1, 5, 0, 3, 2).reshape(512, 64)


def first_twiddle():
    t = angle(np.arange(16)[:, None], np.arange(128)[None, :] % 16, 256)
    return np.concatenate([np.cos(t), np.sin(t)], 0).astype(np.float32)


def first_halves():
    t = angle(np.arange(2)[:, None], np.arange(16)[None, :], 16)
    c, s = np.cos(t), np.sin(t)
    full = np.stack([np.stack([c, -s], 1), np.stack([s, c], 1)], 1)
    return np.einsum("hsrx,ab->hsarbx", full, np.eye(8)).reshape(32, 256)


def first_inverse():
    p = np.arange(32)
    t = angle(frequency(p)[:, None], np.arange(256)[None, :], 256)
    full = np.stack([np.cos(t), np.sin(t)], 0).reshape(2, 16, 2, 256)
    return full.transpose(0, 2, 1, 3).reshape(64, 256)


def split(values):
    high = values.astype(BF16)
    low = (values - high.astype(F32)).astype(BF16)
    return high, low


def dot(a, b, dims=((1,), (0,))):
    return lax.dot_general(a, b, (dims, ((), ())), preferred_element_type=F32)


def dot3(a, b, dims=((1,), (0,))):
    return dot(a[0], b[0], dims) + (dot(a[0], b[1], dims) + dot(a[1], b[0], dims))


def lanes(shape):
    return lax.broadcasted_iota(jnp.int32, shape, len(shape) - 1)


def transpose_groups(blocks, width):
    blocks = list(blocks)
    count = len(blocks)
    group = lanes(blocks[0].shape) // width
    step = 1
    while step < count:
        upper = (group & step) != 0
        for i in range(count):
            if i & step:
                continue
            a, b = blocks[i], blocks[i | step]
            blocks[i] = jnp.where(upper, pltpu.roll(b, step * width, 1), a)
            blocks[i | step] = jnp.where(upper, b, pltpu.roll(a, 128 - step * width, 1))
        step *= 2
    return blocks


def fft(parts):
    count = len(parts)
    if count == 1:
        return parts
    even, odd = fft(parts[0::2]), fft(parts[1::2])
    out = [None] * count
    for j in range(count // 2):
        er, ei = even[j]
        orr, oi = odd[j]
        if j == 0:
            tr, ti = orr, oi
        elif 4 * j == count:
            tr, ti = oi, -orr
        else:
            c, s = math.cos(2 * math.pi * j / count), math.sin(2 * math.pi * j / count)
            tr, ti = orr * c + oi * s, oi * c - orr * s
        out[j] = (er + tr, ei + ti)
        out[j + count // 2] = (er - tr, ei - ti)
    return out


def start_kernel(x_ref, pre_ref, cot_ref, dh_ref, dl_ref, grad_ref, out_ref):
    v = pre_ref[...]
    cumulative = 0.5 * (1.0 + lax.erf(v * (1.0 / math.sqrt(2.0))))
    density = jnp.exp(-0.5 * v * v) * (1.0 / math.sqrt(2.0 * math.pi))
    grad = cot_ref[...] * (cumulative + v * density)
    grad_ref[...] = grad
    table = (dh_ref[...], dl_ref[...])
    for i in range(x_ref.shape[1]):
        rows = jnp.concatenate(
            [x_ref[c, i] for c in range(4)] + [grad[c, i] for c in range(4)], axis=0
        )
        out_ref[i] = dot3(table, split(rows), ((1,), (1,)))


def second_kernel(in_ref, th_ref, tl_ref, out_ref):
    both = jnp.concatenate([th_ref[...], tl_ref[...]], axis=0)
    for k in range(8):
        rows = jnp.concatenate([in_ref[s, 32 * k : 32 * k + 32, :] for s in range(16)], axis=0)
        high, low = split(rows)
        two = dot(both, high)
        done = two[:64] + (two[64:] + dot(th_ref[...], low))
        for ri in range(2):
            for q in range(2):
                j = 2 * ri + q
                out_ref[pl.ds(ri * 16 + k * 2 + q, 16, stride=32), :] = done[16 * j : 16 * j + 16]


def first_kernel(in_ref, tw_ref, bh_ref, bl_ref, mix_ref, out_ref):
    parts = [(in_ref[32 * s : 32 * s + 16], in_ref[32 * s + 16 : 32 * s + 32]) for s in range(16)]
    rows = []
    for r, (re, im) in enumerate(fft(parts)):
        c, s = tw_ref[r : r + 1], tw_ref[16 + r : 17 + r]
        rows.append(jnp.concatenate([re * c + im * s, im * c - re * s], axis=1))
    data = split(jnp.concatenate(rows, axis=0))
    done = dot3((bh_ref[...], bl_ref[...]), data, ((1,), (1,)))
    lane = lanes((16, 128))
    for h in range(2):
        for b in range(8):
            tile = done[16 * h : 16 * h + 16, 128 * (b // 4) : 128 * (b // 4) + 128]
            if b % 4:
                tile = pltpu.roll(tile, 128 - 32 * (b % 4), 1)
            d = 8 * h + b
            mix = mix_ref[16 * (d // 4) : 16 * (d // 4) + 16]
            shift = (32 - 16 * (d % 4)) % 128
            if shift:
                mix = pltpu.roll(mix, shift, 1)
            out_ref[16 * d : 16 * d + 16] = jnp.where(lane < 32, tile, mix)


def swap_halves(b1):
    turned = pltpu.roll(b1, 64, 1)
    return jnp.where(lanes(b1.shape) < 64, turned, -turned)


def mode_kernel(in_ref, w_ref, out_ref, xr_ref, xi_ref, b1_ref, mix_ref):
    def field(ri, f):
        return jnp.concatenate(
            [in_ref[pl.ds(8 * ri + 4 * f + c, 16, stride=16), :] for c in range(4)], axis=0
        )

    spread = jnp.concatenate([field(0, 1), field(1, 1)], axis=0).T[:32]
    mode = lax.broadcasted_iota(jnp.int32, (32, 128), 0)
    b1 = spread * jnp.where((mode // 2) % 8 == 0, 1.0 / CELLS, 2.0 / CELLS)
    b2 = swap_halves(b1)
    lane = lanes((64, 128))
    total = jnp.zeros((64, 128), F32)
    for m in range(32):
        p, k, q = m // 16, (m // 2) % 8, m % 2
        at = ((p * 2 + q) * 8 + k) * 64
        weight = w_ref[at : at + 64]
        place = q + 4 * (k // 2) + 16 * p + 64 * (k % 2)
        real = jnp.sum(weight * b1[m : m + 1], axis=1, keepdims=True)
        imag = jnp.sum(weight * b2[m : m + 1], axis=1, keepdims=True)
        total = jnp.where(lane == place, real, total)
        total = jnp.where(lane == place + 2, imag, total)
    for c in range(4):
        out_ref[pl.ds(c, 16, stride=4), :] = total[16 * c : 16 * c + 16]
    xr_ref[...] = field(0, 0)
    xi_ref[...] = field(1, 0)
    b1_ref[...] = b1
    mix = in_ref[0:16]
    for s in range(1, 16):
        mix = mix + in_ref[16 * s : 16 * s + 16]
    mix_ref[...] = jnp.where(lanes((8, 128)) < 48, mix[:8], pltpu.roll(mix[8:], 16, 1))


def outer_kernel(xr_ref, xi_ref, b1_ref, out_ref):
    xr, xi, b1 = xr_ref[...], xi_ref[...], b1_ref[...]
    b2 = swap_halves(b1)
    for m in range(32):
        p, k, q = m // 16, (m // 2) % 8, m % 2
        at = ((p * 2 + q) * 8 + k) * 64
        out_ref[at : at + 64] = xr[:, m : m + 1] * b1[m : m + 1] + xi[:, m : m + 1] * b2[m : m + 1]


def first_back_kernel(in_ref, t_ref, mix_ref, out_ref):
    parts = [in_ref[pl.ds(c, 16, stride=4), :] for c in range(4)]
    lane = lanes((16, 128))
    rows = []
    for p in range(2):
        merged = None
        for c in range(4):
            shift = (16 * (c - p)) % 128
            moved = pltpu.roll(parts[c], shift, 1) if shift else parts[c]
            merged = moved if merged is None else jnp.where((lane // 16) % 4 == c, moved, merged)
        rows.append(merged)
    re = jnp.concatenate(rows, axis=0)
    turned = jnp.where(
        (lanes((32, 128)) // 2) % 2 == 0, -pltpu.roll(re, 126, 1), pltpu.roll(re, 2, 1)
    )
    high, low = split(jnp.concatenate([re, turned], axis=0))
    done = dot(jnp.concatenate([high, high, low], axis=0), t_ref[...], ((0,), (0,)))
    mix = mix_ref[...]
    for t in range(2):
        blocks = [done[16 * b : 16 * b + 16, 128 * t : 128 * t + 128] for b in range(8)]
        for g, block in enumerate(transpose_groups(blocks, 16)):
            out_ref[8 * t + g, 0:16, :] = block
            out_ref[8 * t + g, 16:24, :] = mix


def second_back_kernel(in_ref, t_ref, out_ref):
    for k in range(4):
        rows = jnp.concatenate(
            [in_ref[pl.ds(4 * k + j, 16, stride=24), :] for j in range(4)], axis=0
        )
        high, low = split(rows)
        done = dot(t_ref[...], jnp.concatenate([high, high, low], axis=0))
        for y in range(16):
            out_ref[y, 32 * k : 32 * k + 32, :] = done[32 * y : 32 * y + 32]
    mix = in_ref[16:24]
    for s in range(1, 16):
        mix = mix + in_ref[24 * s + 16 : 24 * s + 24]
    lane = lanes((8, 128))
    for y in range(16):
        out_ref[y, 16:24, :] = jnp.where(lane < 64, mix, out_ref[y, 16:24, :])


def end_kernel(in_ref, mixed_ref, direct_ref, dh_ref, dl_ref, out_ref, mix_ref):
    table = (dh_ref[...], dl_ref[...])
    for i in range(in_ref.shape[0]):
        turned = in_ref[i].T
        rows = jnp.concatenate([turned[:64], turned[64:]], axis=1)
        done = dot3(split(rows), table)
        for c in range(4):
            out_ref[c, i] = direct_ref[c, i] + done[16 * c : 16 * c + 16]

    @pl.when(pl.program_id(0) == 0)
    def _():
        lane = lanes((8, 128))
        scale = 1.0 / math.sqrt(CELLS)
        for block in range(4):
            for half in range(2):
                total = None
                for o in range(4):
                    part = mixed_ref[4 * block + o]
                    shift = (16 * o - 32 - 16 * half) % 128
                    part = pltpu.roll(part, shift, 1) if shift else part
                    total = part if total is None else jnp.where(lane // 16 == o, part, total)
                at = 16 * block + 8 * half
                mix_ref[at : at + 8, :] = total[:, :64] * scale


def side_kernel(x_ref, grad_ref, weight_ref, direct_ref, mix_ref):
    high, low = split(weight_ref[...])
    weight = jnp.concatenate([high, low, high], axis=1)
    total = jnp.zeros((64, 64), F32)
    for x in range(16):
        field = split(x_ref[:, x, :])
        gh, gl = split(grad_ref[:, x, :])
        total = total + dot3(field, (gh, gl), ((1,), (1,)))
        direct_ref[:, x, :] = dot(weight, jnp.concatenate([gh, gh, gl], axis=0))
    mix_ref[...] = jnp.concatenate([total, total], axis=1)


def params(mebibytes):
    return pltpu.CompilerParams(vmem_limit_bytes=mebibytes << 20)


def whole(count):
    return [pl.BlockSpec(memory_space=pltpu.VMEM)] * count


def struct(*shape):
    return jax.ShapeDtypeStruct(shape, F32)


def call(body, outs, args, mebibytes=16, cost=None):
    many = isinstance(outs, tuple)
    return pl.pallas_call(
        body,
        out_shape=outs,
        in_specs=whole(len(args)),
        out_specs=tuple(whole(len(outs))) if many else whole(1)[0],
        compiler_params=params(mebibytes),
        cost_estimate=cost,
    )(*args)


def exchange(values, axis):
    return lax.all_to_all(values, axis, split_axis=0, concat_axis=0, tiled=True)


def stacked(table):
    high, low = pair(table)
    return np.concatenate([high, low, high], axis=1)


def per_device(inputs, pre_act, cotangent, mix_weight, spectral_weight):
    steps, per = 4, 4
    field_spec = pl.BlockSpec((4, per, 16, 512), lambda i: (0, i, 0, 0))
    table_spec = pl.BlockSpec((256, 512), lambda i: (0, 0))
    shaped = [a.reshape(4, 16, 16, 512) for a in (inputs, pre_act, cotangent)]
    grad_pre, depth = pl.pallas_call(
        start_kernel,
        grid=(steps,),
        out_shape=(struct(4, 16, 16, 512), struct(16, 256, 128)),
        in_specs=[field_spec] * 3 + [table_spec] * 2,
        out_specs=(field_spec, pl.BlockSpec((per, 256, 128), lambda i: (i, 0, 0))),
        compiler_params=params(32),
    )(*shaped, *map(jnp.asarray, pair(depth_forward())))

    depth = exchange(depth, "py")
    direct, mix = call(
        side_kernel,
        (struct(64, 16, 512), struct(64, 128)),
        (inputs, grad_pre.reshape(64, 16, 512), mix_weight),
        24,
        pl.CostEstimate(flops=1 << 30, bytes_accessed=6 << 20, transcendentals=0),
    )
    along_second = call(
        second_kernel, struct(512, 128), (depth, *map(jnp.asarray, pair(second_forward()))), 16
    )
    along_second = exchange(along_second.reshape(16, 32, 128), "px").reshape(512, 128)
    along_first = call(
        first_kernel,
        struct(256, 128),
        (along_second, jnp.asarray(first_twiddle()), *map(jnp.asarray, pair(first_halves())), mix),
    )
    spectra = exchange(along_first.reshape(16, 16, 128), "py").reshape(256, 128)
    mode_back, xr, xi, b1, mix = call(
        mode_kernel,
        (struct(64, 128), struct(64, 128), struct(64, 128), struct(32, 128), struct(8, 128)),
        (spectra, spectral_weight.reshape(2048, 128)),
    )
    mode_back = exchange(mode_back.reshape(16, 4, 128), "py").reshape(64, 128)
    spectral_grad = call(
        outer_kernel,
        struct(2048, 128),
        (xr, xi, b1),
        16,
        pl.CostEstimate(flops=1 << 20, bytes_accessed=1 << 20, transcendentals=0),
    ).reshape(spectral_weight.shape)
    first_high, first_low = pair(first_inverse())
    first_table = np.concatenate([first_high, first_low, first_high], axis=0)
    first_back = call(
        first_back_kernel, struct(16, 24, 128), (mode_back, jnp.asarray(first_table), mix)
    )
    first_back = exchange(first_back, "px").reshape(384, 128)
    second_back = call(
        second_back_kernel,
        struct(16, 128, 128),
        (first_back, jnp.asarray(stacked(second_inverse()))),
    )
    gathered = exchange(second_back, "py")
    input_grad, mix_grad = pl.pallas_call(
        end_kernel,
        grid=(steps,),
        out_shape=(struct(4, 16, 16, 512), struct(64, 64)),
        in_specs=[
            pl.BlockSpec((per, 128, 128), lambda i: (i, 0, 0)),
            pl.BlockSpec((16, 8, 128), lambda i: (0, 2, 0)),
            field_spec,
            table_spec,
            table_spec,
        ],
        out_specs=(field_spec, pl.BlockSpec((64, 64), lambda i: (0, 0))),
        compiler_params=params(24),
    )(
        gathered,
        gathered,
        direct.reshape(4, 16, 16, 512),
        *map(jnp.asarray, pair(depth_inverse())),
    )
    return (input_grad.reshape(inputs.shape), spectral_grad, mix_grad)


def solution(mesh):
    placed = (
        P(None, "px", "py"),
        P(None, "px", "py"),
        P(None, "px", "py"),
        P(),
        P("py", "px", None, None, None),
    )
    return jax.shard_map(
        per_device,
        mesh=mesh,
        in_specs=placed,
        out_specs=(P(None, "px", "py"), P("py", "px", None, None, None), P()),
        check_vma=False,
    )
```

```python
import math

import jax
import jax.numpy as jnp
import ml_dtypes
import numpy as np
from jax import lax
from jax.experimental import pallas as pl
from jax.experimental.pallas import tpu as pltpu
from jax.sharding import PartitionSpec as P

C = 64
NX = 256
NY = 256
NZ = 32
MZ = 8
CELLS = NX * NY * NZ
N = 16
F32 = jnp.float32
BF16 = jnp.bfloat16


def pair(table):
    high = table.astype(ml_dtypes.bfloat16)
    low = (table - high.astype(np.float64)).astype(high.dtype)
    return high, low


def column(table):
    return jnp.asarray(np.concatenate(pair(table), axis=0))


def frequency(index):
    return np.where(index < 16, index, index - 32)


def angle(a, b, length):
    return 2.0 * np.pi / length * np.mod(a * b, length)


def depth_forward():
    k, z = np.arange(8)[:, None], np.arange(32)[None, :]
    t = angle(k, z, 32)
    parts = np.stack([np.cos(t), -np.sin(t)], 1)
    return np.einsum("krz,ab->krabz", parts, np.eye(16)).reshape(256, 512)


def depth_inverse():
    return depth_forward().reshape(4, 2, 2, 16, 512).transpose(1, 0, 2, 3, 4).reshape(256, 512)


def second_forward():
    q = np.arange(32)
    t = angle(frequency(q)[:, None], np.arange(256)[None, :], 256)
    c, s = np.cos(t), np.sin(t)
    full = np.stack([np.stack([c, s], 1), np.stack([-s, c], 1)], 0)
    full = full.reshape(2, 16, 2, 2, 16, 16)
    return full.transpose(0, 2, 1, 4, 3, 5).reshape(64, 512)


def second_inverse():
    q = np.arange(32)
    t = angle(frequency(q)[:, None], np.arange(256)[None, :], 256)
    c, s = np.cos(t), np.sin(t)
    full = np.stack([np.stack([c, s], 0), np.stack([-s, c], 0)], 0)
    full = full.reshape(2, 2, 16, 2, 16, 16)
    return full.transpose(4, 1, 5, 0, 3, 2).reshape(512, 64)


def first_twiddle():
    t = angle(np.arange(16)[:, None], np.arange(128)[None, :] % 16, 256)
    return np.concatenate([np.cos(t), np.sin(t)], 0).astype(np.float32)


def first_halves():
    t = angle(np.arange(2)[:, None], np.arange(16)[None, :], 16)
    c, s = np.cos(t), np.sin(t)
    full = np.stack([np.stack([c, -s], 1), np.stack([s, c], 1)], 1)
    return np.einsum("hsrx,ab->hsarbx", full, np.eye(8)).reshape(32, 256)


def first_inverse():
    p = np.arange(32)
    t = angle(frequency(p)[:, None], np.arange(256)[None, :], 256)
    full = np.stack([np.cos(t), np.sin(t)], 0).reshape(2, 16, 2, 256)
    return full.transpose(0, 2, 1, 3).reshape(64, 256)


def split(values):
    high = values.astype(BF16)
    low = (values - high.astype(F32)).astype(BF16)
    return high, low


def dot(a, b, dims=((1,), (0,))):
    return lax.dot_general(a, b, (dims, ((), ())), preferred_element_type=F32)


def dot3(a, b, dims=((1,), (0,))):
    return dot(a[0], b[0], dims) + (dot(a[0], b[1], dims) + dot(a[1], b[0], dims))


def lanes(shape):
    return lax.broadcasted_iota(jnp.int32, shape, len(shape) - 1)


def transpose_groups(blocks, width):
    blocks = list(blocks)
    count = len(blocks)
    group = lanes(blocks[0].shape) // width
    step = 1
    while step < count:
        upper = (group & step) != 0
        for i in range(count):
            if i & step:
                continue
            a, b = blocks[i], blocks[i | step]
            blocks[i] = jnp.where(upper, pltpu.roll(b, step * width, 1), a)
            blocks[i | step] = jnp.where(upper, b, pltpu.roll(a, 128 - step * width, 1))
        step *= 2
    return blocks


def fft(parts):
    count = len(parts)
    if count == 1:
        return parts
    even, odd = fft(parts[0::2]), fft(parts[1::2])
    out = [None] * count
    for j in range(count // 2):
        er, ei = even[j]
        orr, oi = odd[j]
        if j == 0:
            tr, ti = orr, oi
        elif 4 * j == count:
            tr, ti = oi, -orr
        else:
            c, s = math.cos(2 * math.pi * j / count), math.sin(2 * math.pi * j / count)
            tr, ti = orr * c + oi * s, oi * c - orr * s
        out[j] = (er + tr, ei + ti)
        out[j + count // 2] = (er - tr, ei - ti)
    return out


def start_kernel(x_ref, pre_ref, cot_ref, table_ref, grad_ref, out_ref):
    v = pre_ref[...]
    cumulative = 0.5 * (1.0 + lax.erf(v * (1.0 / math.sqrt(2.0))))
    density = jnp.exp(-0.5 * v * v) * (1.0 / math.sqrt(2.0 * math.pi))
    grad = cot_ref[...] * (cumulative + v * density)
    grad_ref[...] = grad
    table = (table_ref[:256], table_ref[256:])
    for i in range(x_ref.shape[1]):
        rows = jnp.concatenate(
            [x_ref[c, i] for c in range(4)] + [grad[c, i] for c in range(4)], axis=0
        )
        out_ref[i] = dot3(table, split(rows), ((1,), (1,)))


def second_kernel(in_ref, table_ref, out_ref):
    both = table_ref[...]
    for k in range(8):
        rows = jnp.concatenate([in_ref[s, 32 * k : 32 * k + 32, :] for s in range(16)], axis=0)
        high, low = split(rows)
        two = dot(both, high)
        done = two[:64] + (two[64:] + dot(both[:64], low))
        for ri in range(2):
            for q in range(2):
                j = 2 * ri + q
                out_ref[pl.ds(ri * 16 + k * 2 + q, 16, stride=32), :] = done[16 * j : 16 * j + 16]


def first_kernel(in_ref, tw_ref, table_ref, mix_ref, out_ref):
    parts = [(in_ref[32 * s : 32 * s + 16], in_ref[32 * s + 16 : 32 * s + 32]) for s in range(16)]
    rows = []
    for r, (re, im) in enumerate(fft(parts)):
        c, s = tw_ref[r : r + 1], tw_ref[16 + r : 17 + r]
        rows.append(jnp.concatenate([re * c + im * s, im * c - re * s], axis=1))
    data = split(jnp.concatenate(rows, axis=0))
    done = dot3((table_ref[:32], table_ref[32:]), data, ((1,), (1,)))
    for h in range(2):
        for b in range(8):
            tile = done[16 * h : 16 * h + 16, 128 * (b // 4) : 128 * (b // 4) + 128]
            if b % 4:
                tile = pltpu.roll(tile, 128 - 32 * (b % 4), 1)
            d = 8 * h + b
            out_ref[16 * d : 16 * d + 16] = tile
            out_ref[16 * d : 16 * d + 4, 64:128] = mix_ref[4 * d : 4 * d + 4, 64:128]


def swap_halves(b1):
    turned = pltpu.roll(b1, 64, 1)
    return jnp.where(lanes(b1.shape) < 64, turned, -turned)


def mode_kernel(in_ref, w_ref, out_ref, xr_ref, xi_ref, b1_ref, mix_ref):
    def field(ri, f):
        return jnp.concatenate(
            [in_ref[pl.ds(8 * ri + 4 * f + c, 16, stride=16), :] for c in range(4)], axis=0
        )

    spread = jnp.concatenate([field(0, 1), field(1, 1)], axis=0).T[:32]
    mode = lax.broadcasted_iota(jnp.int32, (32, 128), 0)
    b1 = spread * jnp.where((mode // 2) % 8 == 0, 1.0 / CELLS, 2.0 / CELLS)
    b2 = swap_halves(b1)
    lane = lanes((64, 128))
    total = jnp.zeros((64, 128), F32)
    for m in range(32):
        p, k, q = m // 16, (m // 2) % 8, m % 2
        at = ((p * 2 + q) * 8 + k) * 64
        weight = w_ref[at : at + 64]
        place = q + 4 * (k // 2) + 16 * p + 64 * (k % 2)
        real = jnp.sum(weight * b1[m : m + 1], axis=1, keepdims=True)
        imag = jnp.sum(weight * b2[m : m + 1], axis=1, keepdims=True)
        total = jnp.where(lane == place, real, total)
        total = jnp.where(lane == place + 2, imag, total)
    for c in range(4):
        out_ref[pl.ds(c, 16, stride=4), :] = total[16 * c : 16 * c + 16]
    xr_ref[...] = field(0, 0)
    xi_ref[...] = field(1, 0)
    b1_ref[...] = b1
    mix = in_ref[0:4]
    for s in range(1, 16):
        mix = mix + in_ref[16 * s : 16 * s + 4]
    mix_ref[...] = jnp.where(lanes((2, 128)) < 64, pltpu.roll(mix, 64, 1)[:2], mix[2:])


def outer_kernel(xr_ref, xi_ref, b1_ref, out_ref):
    xr, xi, b1 = xr_ref[...], xi_ref[...], b1_ref[...]
    b2 = swap_halves(b1)
    for m in range(32):
        p, k, q = m // 16, (m // 2) % 8, m % 2
        at = ((p * 2 + q) * 8 + k) * 64
        out_ref[at : at + 64] = xr[:, m : m + 1] * b1[m : m + 1] + xi[:, m : m + 1] * b2[m : m + 1]


def first_back_kernel(in_ref, t_ref, mix_ref, out_ref):
    parts = [in_ref[pl.ds(c, 16, stride=4), :] for c in range(4)]
    lane = lanes((16, 128))
    rows = []
    for p in range(2):
        merged = None
        for c in range(4):
            shift = (16 * (c - p)) % 128
            moved = pltpu.roll(parts[c], shift, 1) if shift else parts[c]
            merged = moved if merged is None else jnp.where((lane // 16) % 4 == c, moved, merged)
        rows.append(merged)
    re = jnp.concatenate(rows, axis=0)
    turned = jnp.where(
        (lanes((32, 128)) // 2) % 2 == 0, -pltpu.roll(re, 126, 1), pltpu.roll(re, 2, 1)
    )
    high, low = split(jnp.concatenate([re, turned], axis=0))
    done = dot(jnp.concatenate([high, high, low], axis=0), t_ref[...], ((0,), (0,)))
    mix = mix_ref[...]
    for t in range(2):
        blocks = [done[16 * b : 16 * b + 16, 128 * t : 128 * t + 128] for b in range(8)]
        for g, block in enumerate(transpose_groups(blocks, 16)):
            at = 18 * (8 * t + g)
            out_ref[at : at + 16] = block
            out_ref[at + 16 : at + 18] = mix


def second_back_kernel(in_ref, t_ref, out_ref):
    for k in range(4):
        rows = jnp.concatenate(
            [in_ref[pl.ds(4 * k + j, 16, stride=18), :] for j in range(4)], axis=0
        )
        high, low = split(rows)
        done = dot(t_ref[...], jnp.concatenate([high, high, low], axis=0))
        for y in range(16):
            out_ref[y, 32 * k : 32 * k + 32, :] = done[32 * y : 32 * y + 32]
    mix = in_ref[16:18]
    for s in range(1, 16):
        mix = mix + in_ref[18 * s + 16 : 18 * s + 18]
    mix = jnp.concatenate([mix, pltpu.roll(mix, 64, 1)], axis=0)
    for y in range(16):
        out_ref[y, 16:20, 0:64] = mix[:, :64]


def end_kernel(in_ref, mixed_ref, direct_ref, table_ref, out_ref, mix_ref):
    table = (table_ref[:256], table_ref[256:])
    for i in range(in_ref.shape[0]):
        turned = in_ref[i].T
        rows = jnp.concatenate([turned[:64], turned[64:]], axis=1)
        done = dot3(split(rows), table)
        for c in range(4):
            out_ref[c, i] = direct_ref[c, i] + done[16 * c : 16 * c + 16]

    @pl.when(pl.program_id(0) == 0)
    def _():
        for d in range(16):
            mix_ref[4 * d : 4 * d + 4] = mixed_ref[d, 0:4, 0:64] * (1.0 / math.sqrt(CELLS))


def side_kernel(x_ref, grad_ref, weight_ref, direct_ref, mix_ref):
    high, low = split(weight_ref[...])
    weight = jnp.concatenate([high, low, high], axis=1)
    total = jnp.zeros((64, 64), F32)
    for x in range(16):
        field = split(x_ref[pl.ds(x, 64, stride=16), :])
        gh, gl = split(grad_ref[pl.ds(x, 64, stride=16), :])
        total = total + dot3(field, (gh, gl), ((1,), (1,)))
        direct_ref[pl.ds(x, 64, stride=16), :] = dot(weight, jnp.concatenate([gh, gh, gl], axis=0))
    total = jnp.concatenate([total, total], axis=1)
    first = pl.program_id(0) == 0

    @pl.when(first)
    def _():
        mix_ref[...] = total

    @pl.when(jnp.logical_not(first))
    def _():
        mix_ref[...] += total


def params(mebibytes):
    return pltpu.CompilerParams(vmem_limit_bytes=mebibytes << 20)


def whole(count):
    return [pl.BlockSpec(memory_space=pltpu.VMEM)] * count


def struct(*shape):
    return jax.ShapeDtypeStruct(shape, F32)


def call(body, outs, args, mebibytes=12, cost=None):
    many = isinstance(outs, tuple)
    return pl.pallas_call(
        body,
        out_shape=outs,
        in_specs=whole(len(args)),
        out_specs=tuple(whole(len(outs))) if many else whole(1)[0],
        compiler_params=params(mebibytes),
        cost_estimate=cost,
    )(*args)


def exchange(values, axis):
    return lax.all_to_all(values, axis, split_axis=0, concat_axis=0, tiled=True)


def stacked(table):
    high, low = pair(table)
    return np.concatenate([high, low, high], axis=1)


def per_device(inputs, pre_act, cotangent, mix_weight, spectral_weight):
    steps, per = 8, 2
    field_spec = pl.BlockSpec((4, per, 16, 512), lambda i: (0, i, 0, 0))
    table_spec = pl.BlockSpec((512, 512), lambda i: (0, 0))
    shaped = [a.reshape(4, 16, 16, 512) for a in (inputs, pre_act, cotangent)]
    grad_pre, depth = pl.pallas_call(
        start_kernel,
        grid=(steps,),
        out_shape=(struct(4, 16, 16, 512), struct(16, 256, 128)),
        in_specs=[field_spec] * 3 + [table_spec],
        out_specs=(field_spec, pl.BlockSpec((per, 256, 128), lambda i: (i, 0, 0))),
        compiler_params=params(60),
    )(*shaped, column(depth_forward()))

    tile_spec = pl.BlockSpec((1024, 128), lambda i: (0, i))
    direct, mix = pl.pallas_call(
        side_kernel,
        grid=(4,),
        out_shape=(struct(1024, 512), struct(64, 128)),
        in_specs=[tile_spec, tile_spec, pl.BlockSpec((64, 64), lambda i: (0, 0))],
        out_specs=(tile_spec, pl.BlockSpec((64, 128), lambda i: (0, 0))),
        compiler_params=params(60),
        cost_estimate=pl.CostEstimate(flops=1 << 30, bytes_accessed=6 << 20, transcendentals=0),
    )(inputs.reshape(1024, 512), grad_pre.reshape(1024, 512), mix_weight)
    depth, direct, mix = lax.optimization_barrier((exchange(depth, "py"), direct, mix))
    along_second = call(
        second_kernel, struct(512, 128), (depth, column(second_forward()))
    )
    along_second = exchange(along_second.reshape(16, 32, 128), "px").reshape(512, 128)
    along_first = call(
        first_kernel,
        struct(256, 128),
        (along_second, jnp.asarray(first_twiddle()), column(first_halves()), mix),
    )
    spectra = exchange(along_first.reshape(16, 16, 128), "py").reshape(256, 128)
    mode_back, xr, xi, b1, mix = call(
        mode_kernel,
        (struct(64, 128), struct(64, 128), struct(64, 128), struct(32, 128), struct(2, 128)),
        (spectra, spectral_weight.reshape(2048, 128)),
    )
    mode_back = exchange(mode_back.reshape(16, 4, 128), "py").reshape(64, 128)
    spectral_grad = call(
        outer_kernel,
        struct(2048, 128),
        (xr, xi, b1),
        8,
        pl.CostEstimate(flops=1 << 20, bytes_accessed=1 << 20, transcendentals=0),
    ).reshape(spectral_weight.shape)
    first_high, first_low = pair(first_inverse())
    first_table = np.concatenate([first_high, first_low, first_high], axis=0)
    first_back = call(
        first_back_kernel, struct(288, 128), (mode_back, jnp.asarray(first_table), mix)
    )
    first_back = exchange(first_back.reshape(16, 1, 2304), "px").reshape(288, 128)
    second_back = call(
        second_back_kernel,
        struct(16, 128, 128),
        (first_back, jnp.asarray(stacked(second_inverse()))),
    )
    gathered = exchange(second_back, "py")
    input_grad, mix_grad = pl.pallas_call(
        end_kernel,
        grid=(steps,),
        out_shape=(struct(4, 16, 16, 512), struct(64, 64)),
        in_specs=[
            pl.BlockSpec((per, 128, 128), lambda i: (i, 0, 0)),
            pl.BlockSpec((16, 8, 128), lambda i: (0, 2, 0)),
            field_spec,
            table_spec,
        ],
        out_specs=(field_spec, pl.BlockSpec((64, 64), lambda i: (0, 0))),
        compiler_params=params(24),
    )(
        gathered,
        gathered,
        direct.reshape(4, 16, 16, 512),
        column(depth_inverse()),
    )
    return (input_grad.reshape(inputs.shape), spectral_grad, mix_grad)


def solution(mesh):
    placed = (
        P(None, "px", "py"),
        P(None, "px", "py"),
        P(None, "px", "py"),
        P(),
        P("py", "px", None, None, None),
    )
    return jax.shard_map(
        per_device,
        mesh=mesh,
        in_specs=placed,
        out_specs=(P(None, "px", "py"), P("py", "px", None, None, None), P()),
        check_vma=False,
    )
```

```python
import math

import jax
import jax.numpy as jnp
import ml_dtypes
import numpy as np
from jax import lax
from jax.experimental import pallas as pl
from jax.experimental.pallas import tpu as pltpu
from jax.sharding import PartitionSpec as P

C = 64
NX = 256
NY = 256
NZ = 32
MZ = 8
CELLS = NX * NY * NZ
N = 16
ROWS = 240
PER = 2
PARTS = N // PER
F32 = jnp.float32
BF16 = jnp.bfloat16


def pair(table):
    high = table.astype(ml_dtypes.bfloat16)
    low = (table - high.astype(np.float64)).astype(high.dtype)
    return high, low


def column(table):
    return jnp.asarray(np.concatenate(pair(table), axis=0))


def frequency(index):
    return np.where(index < 16, index, index - 32)


def angle(a, b, length):
    return 2.0 * np.pi / length * np.mod(a * b, length)


def depth_forward():
    k, z = np.arange(8)[:, None], np.arange(32)[None, :]
    t = angle(k, z, 32)
    parts = np.stack([np.cos(t), -np.sin(t)], 1)
    return np.einsum("krz,ab->krabz", parts, np.eye(16)).reshape(256, 512)


def depth_sent():
    return np.delete(depth_forward(), np.arange(16, 32), axis=0)


def depth_inverse():
    return depth_forward().reshape(4, 2, 2, 16, 512).transpose(1, 0, 2, 3, 4).reshape(256, 512)


def second_forward():
    q = np.arange(32)
    t = angle(frequency(q)[:, None], np.arange(256)[None, :], 256)
    c, s = np.cos(t), np.sin(t)
    full = np.stack([np.stack([c, s], 1), np.stack([-s, c], 1)], 0)
    full = full.reshape(2, 16, 2, 2, 16, 16)
    return full.transpose(0, 2, 1, 4, 3, 5).reshape(64, 512)


def second_real():
    return second_forward().reshape(64, 16, 2, 16)[:, :, 0].reshape(64, 256)


def second_inverse():
    q = np.arange(32)
    t = angle(frequency(q)[:, None], np.arange(256)[None, :], 256)
    c, s = np.cos(t), np.sin(t)
    full = np.stack([np.stack([c, s], 0), np.stack([-s, c], 0)], 0)
    full = full.reshape(2, 2, 16, 2, 16, 16)
    return full.transpose(4, 1, 5, 0, 3, 2).reshape(512, 64)


def first_twiddle():
    t = angle(np.arange(16)[:, None], np.arange(128)[None, :] % 16, 256)
    return np.concatenate([np.cos(t), np.sin(t)], 0).astype(np.float32)


def first_halves():
    t = angle(np.arange(2)[:, None], np.arange(16)[None, :], 16)
    c, s = np.cos(t), np.sin(t)
    full = np.stack([np.stack([c, -s], 1), np.stack([s, c], 1)], 1)
    return np.einsum("hsrx,ab->hsarbx", full, np.eye(8)).reshape(32, 256)


def first_inverse():
    p = np.arange(32)
    t = angle(frequency(p)[:, None], np.arange(256)[None, :], 256)
    full = np.stack([np.cos(t), np.sin(t)], 0).reshape(2, 16, 2, 256)
    return full.transpose(0, 2, 1, 3).reshape(64, 256)


def split(values):
    high = values.astype(BF16)
    low = (values - high.astype(F32)).astype(BF16)
    return high, low


def dot(a, b, dims=((1,), (0,))):
    return lax.dot_general(a, b, (dims, ((), ())), preferred_element_type=F32)


def dot3(a, b, dims=((1,), (0,))):
    return dot(a[0], b[0], dims) + (dot(a[0], b[1], dims) + dot(a[1], b[0], dims))


def lanes(shape):
    return lax.broadcasted_iota(jnp.int32, shape, len(shape) - 1)


def transpose_groups(blocks, width):
    blocks = list(blocks)
    count = len(blocks)
    group = lanes(blocks[0].shape) // width
    step = 1
    while step < count:
        upper = (group & step) != 0
        for i in range(count):
            if i & step:
                continue
            a, b = blocks[i], blocks[i | step]
            blocks[i] = jnp.where(upper, pltpu.roll(b, step * width, 1), a)
            blocks[i | step] = jnp.where(upper, b, pltpu.roll(a, 128 - step * width, 1))
        step *= 2
    return blocks


def fft(parts):
    count = len(parts)
    if count == 1:
        return parts
    even, odd = fft(parts[0::2]), fft(parts[1::2])
    out = [None] * count
    for j in range(count // 2):
        er, ei = even[j]
        orr, oi = odd[j]
        if j == 0:
            tr, ti = orr, oi
        elif 4 * j == count:
            tr, ti = oi, -orr
        else:
            c, s = math.cos(2 * math.pi * j / count), math.sin(2 * math.pi * j / count)
            tr, ti = orr * c + oi * s, oi * c - orr * s
        out[j] = (er + tr, ei + ti)
        out[j + count // 2] = (er - tr, ei - ti)
    return out


def slope(v):
    cumulative = 0.5 * (1.0 + lax.erf(v * (1.0 / math.sqrt(2.0))))
    density = jnp.exp(-0.5 * v * v) * (1.0 / math.sqrt(2.0 * math.pi))
    return cumulative + v * density


def start_kernel(x_hbm, pre_hbm, cot_hbm, table_ref, out_hbm, x, pre, cot, out, in_sems, out_sems):
    moves = []
    for i in range(PARTS):
        at = pl.ds(PER * i, PER)
        three = [
            pltpu.make_async_copy(a.at[:, at], b.at[:, at], in_sems.at[n, i])
            for n, (a, b) in enumerate([(pre_hbm, pre), (cot_hbm, cot), (x_hbm, x)])
        ]
        for move in three:
            move.start()
        moves.append(three)
    table = (table_ref[:ROWS], table_ref[ROWS:])
    sends = []
    for i in range(PARTS):
        for move in moves[i]:
            move.wait()
        own = slice(PER * i, PER * i + PER)
        grad = cot[:, own] * slope(pre[:, own])
        rows = []
        for j in range(PER):
            rows += [x[c, PER * i + j] for c in range(4)] + [grad[c, j] for c in range(4)]
        done = dot3(table, split(jnp.concatenate(rows, axis=0)), ((1,), (1,)))
        for j in range(PER):
            out[PER * i + j] = done[:, 128 * j : 128 * j + 128]
        at = pl.ds(PER * i, PER)
        send = pltpu.make_async_copy(out.at[at], out_hbm.at[at], out_sems.at[i])
        send.start()
        sends.append(send)
    for send in sends:
        send.wait()


def second_kernel(in_ref, table_ref, real_ref, out_ref):
    for k in range(8):
        at, size = (0, 16) if k == 0 else (32 * k - 16, 32)
        both = real_ref[...] if k == 0 else table_ref[...]
        rows = jnp.concatenate([in_ref[s, at : at + size, :] for s in range(16)], axis=0)
        high, low = split(rows)
        two = dot(both, high)
        done = two[:64] + (two[64:] + dot(both[:64], low))
        for ri in range(2):
            for q in range(2):
                j = 2 * ri + q
                out_ref[pl.ds(ri * 16 + k * 2 + q, 16, stride=32), :] = done[16 * j : 16 * j + 16]


def first_kernel(in_ref, tw_ref, table_ref, mix_ref, out_ref):
    parts = [(in_ref[32 * s : 32 * s + 16], in_ref[32 * s + 16 : 32 * s + 32]) for s in range(16)]
    rows = []
    for r, (re, im) in enumerate(fft(parts)):
        c, s = tw_ref[r : r + 1], tw_ref[16 + r : 17 + r]
        rows.append(jnp.concatenate([re * c + im * s, im * c - re * s], axis=1))
    data = split(jnp.concatenate(rows, axis=0))
    done = dot3((table_ref[:32], table_ref[32:]), data, ((1,), (1,)))
    for h in range(2):
        for b in range(8):
            tile = done[16 * h : 16 * h + 16, 128 * (b // 4) : 128 * (b // 4) + 128]
            if b % 4:
                tile = pltpu.roll(tile, 128 - 32 * (b % 4), 1)
            d = 8 * h + b
            out_ref[16 * d : 16 * d + 16] = tile
            out_ref[16 * d : 16 * d + 4, 64:128] = mix_ref[4 * d : 4 * d + 4, 64:128]


def swap_halves(b1):
    turned = pltpu.roll(b1, 64, 1)
    return jnp.where(lanes(b1.shape) < 64, turned, -turned)


def mode_kernel(in_ref, w_ref, out_ref, xr_ref, xi_ref, b1_ref, mix_ref):
    def field(ri, f):
        return jnp.concatenate(
            [in_ref[pl.ds(8 * ri + 4 * f + c, 16, stride=16), :] for c in range(4)], axis=0
        )

    spread = jnp.concatenate([field(0, 1), field(1, 1)], axis=0).T[:32]
    mode = lax.broadcasted_iota(jnp.int32, (32, 128), 0)
    b1 = spread * jnp.where((mode // 2) % 8 == 0, 1.0 / CELLS, 2.0 / CELLS)
    b2 = swap_halves(b1)
    lane = lanes((64, 128))
    total = jnp.zeros((64, 128), F32)
    for m in range(32):
        p, k, q = m // 16, (m // 2) % 8, m % 2
        at = ((p * 2 + q) * 8 + k) * 64
        weight = w_ref[at : at + 64]
        place = q + 4 * (k // 2) + 16 * p + 64 * (k % 2)
        real = jnp.sum(weight * b1[m : m + 1], axis=1, keepdims=True)
        imag = jnp.sum(weight * b2[m : m + 1], axis=1, keepdims=True)
        total = jnp.where(lane == place, real, total)
        total = jnp.where(lane == place + 2, imag, total)
    for c in range(4):
        out_ref[pl.ds(c, 16, stride=4), :] = total[16 * c : 16 * c + 16]
    xr_ref[...] = field(0, 0)
    xi_ref[...] = field(1, 0)
    b1_ref[...] = b1
    mix = in_ref[0:4]
    for s in range(1, 16):
        mix = mix + in_ref[16 * s : 16 * s + 4]
    mix_ref[...] = jnp.where(lanes((2, 128)) < 64, pltpu.roll(mix, 64, 1)[:2], mix[2:])


def outer_kernel(xr_ref, xi_ref, b1_ref, out_ref):
    xr, xi, b1 = xr_ref[...], xi_ref[...], b1_ref[...]
    b2 = swap_halves(b1)
    for m in range(32):
        p, k, q = m // 16, (m // 2) % 8, m % 2
        at = ((p * 2 + q) * 8 + k) * 64
        out_ref[at : at + 64] = xr[:, m : m + 1] * b1[m : m + 1] + xi[:, m : m + 1] * b2[m : m + 1]


def first_back_kernel(in_ref, t_ref, mix_ref, out_ref):
    parts = [in_ref[pl.ds(c, 16, stride=4), :] for c in range(4)]
    lane = lanes((16, 128))
    rows = []
    for p in range(2):
        merged = None
        for c in range(4):
            shift = (16 * (c - p)) % 128
            moved = pltpu.roll(parts[c], shift, 1) if shift else parts[c]
            merged = moved if merged is None else jnp.where((lane // 16) % 4 == c, moved, merged)
        rows.append(merged)
    re = jnp.concatenate(rows, axis=0)
    turned = jnp.where(
        (lanes((32, 128)) // 2) % 2 == 0, -pltpu.roll(re, 126, 1), pltpu.roll(re, 2, 1)
    )
    high, low = split(jnp.concatenate([re, turned], axis=0))
    done = dot(jnp.concatenate([high, high, low], axis=0), t_ref[...], ((0,), (0,)))
    mix = mix_ref[...]
    for t in range(2):
        blocks = [done[16 * b : 16 * b + 16, 128 * t : 128 * t + 128] for b in range(8)]
        for g, block in enumerate(transpose_groups(blocks, 16)):
            at = 18 * (8 * t + g)
            out_ref[at : at + 16] = block
            out_ref[at + 16 : at + 18] = mix


def second_back_kernel(in_ref, t_ref, out_ref):
    for k in range(4):
        rows = jnp.concatenate(
            [in_ref[pl.ds(4 * k + j, 16, stride=18), :] for j in range(4)], axis=0
        )
        high, low = split(rows)
        done = dot(t_ref[...], jnp.concatenate([high, high, low], axis=0))
        for y in range(16):
            out_ref[y, 32 * k : 32 * k + 32, :] = done[32 * y : 32 * y + 32]
    mix = in_ref[16:18]
    for s in range(1, 16):
        mix = mix + in_ref[18 * s + 16 : 18 * s + 18]
    mix = jnp.concatenate([mix, pltpu.roll(mix, 64, 1)], axis=0)
    for y in range(16):
        out_ref[y, 16:20, 0:64] = mix[:, :64]


def end_kernel(
    in_ref, direct_hbm, table_hbm, out_hbm, mix_hbm, direct, table, out, mix, sems, in_sems, out_sems
):
    table_move = pltpu.make_async_copy(table_hbm, table, sems.at[0])
    table_move.start()
    moves = []
    for i in range(PARTS):
        at = pl.ds(PER * i, PER)
        move = pltpu.make_async_copy(direct_hbm.at[:, at], direct.at[:, at], in_sems.at[i])
        move.start()
        moves.append(move)
    for d in range(16):
        mix[4 * d : 4 * d + 4] = in_ref[d, 16:20, 0:64] * (1.0 / math.sqrt(CELLS))
    mix_move = pltpu.make_async_copy(mix, mix_hbm, sems.at[1])
    mix_move.start()
    sends = []
    for i in range(PARTS):
        rows = []
        for j in range(PER):
            turned = in_ref[PER * i + j].T
            rows.append(jnp.concatenate([turned[:64], turned[64:]], axis=1))
        halves = split(jnp.concatenate(rows, axis=0))
        if i == 0:
            table_move.wait()
        done = dot3(halves, (table[:256], table[256:]))
        moves[i].wait()
        for j in range(PER):
            for c in range(4):
                at = 64 * j + 16 * c
                out[c, PER * i + j] = direct[c, PER * i + j] + done[at : at + 16]
        at = pl.ds(PER * i, PER)
        send = pltpu.make_async_copy(out.at[:, at], out_hbm.at[:, at], out_sems.at[i])
        send.start()
        sends.append(send)
    for send in sends:
        send.wait()
    mix_move.wait()


def side_kernel(x_ref, pre_ref, cot_ref, weight_ref, direct_ref, mix_ref):
    high, low = split(weight_ref[...])
    weight = jnp.concatenate([high, low, high], axis=1)
    total = jnp.zeros((64, 64), F32)
    for x in range(16):
        field = split(x_ref[pl.ds(x, 64, stride=16), :])
        at = pl.ds(x, 64, stride=16)
        gh, gl = split(cot_ref[at, :] * slope(pre_ref[at, :]))
        total = total + dot3(field, (gh, gl), ((1,), (1,)))
        direct_ref[pl.ds(x, 64, stride=16), :] = dot(weight, jnp.concatenate([gh, gh, gl], axis=0))
    total = jnp.concatenate([total, total], axis=1)
    first = pl.program_id(0) == 0

    @pl.when(first)
    def _():
        mix_ref[...] = total

    @pl.when(jnp.logical_not(first))
    def _():
        mix_ref[...] += total


def params(mebibytes):
    return pltpu.CompilerParams(vmem_limit_bytes=mebibytes << 20)


def whole(count):
    return [pl.BlockSpec(memory_space=pltpu.VMEM)] * count


def struct(*shape):
    return jax.ShapeDtypeStruct(shape, F32)


def call(body, outs, args, mebibytes=12, cost=None):
    many = isinstance(outs, tuple)
    return pl.pallas_call(
        body,
        out_shape=outs,
        in_specs=whole(len(args)),
        out_specs=tuple(whole(len(outs))) if many else whole(1)[0],
        compiler_params=params(mebibytes),
        cost_estimate=cost,
    )(*args)


def exchange(values, axis):
    return lax.all_to_all(values, axis, split_axis=0, concat_axis=0, tiled=True)


def stacked(table):
    high, low = pair(table)
    return np.concatenate([high, low, high], axis=1)


def per_device(inputs, pre_act, cotangent, mix_weight, spectral_weight):
    anywhere = pl.BlockSpec(memory_space=pl.ANY)
    field = pltpu.VMEM((4, N, N, 512), F32)
    shaped = [a.reshape(4, N, N, 512) for a in (inputs, pre_act, cotangent)]
    depth = pl.pallas_call(
        start_kernel,
        out_shape=struct(N, ROWS, 128),
        in_specs=[anywhere] * 3 + whole(1),
        out_specs=anywhere,
        scratch_shapes=[
            field,
            field,
            field,
            pltpu.VMEM((N, ROWS, 128), F32),
            pltpu.SemaphoreType.DMA((3, PARTS)),
            pltpu.SemaphoreType.DMA((PARTS,)),
        ],
        compiler_params=params(60),
    )(*shaped, column(depth_sent()))

    tile_spec = pl.BlockSpec((1024, 128), lambda i: (0, i))
    direct, mix = pl.pallas_call(
        side_kernel,
        grid=(4,),
        out_shape=(struct(1024, 512), struct(64, 128)),
        in_specs=[tile_spec] * 3 + [pl.BlockSpec((64, 64), lambda i: (0, 0))],
        out_specs=(tile_spec, pl.BlockSpec((64, 128), lambda i: (0, 0))),
        compiler_params=params(60),
        cost_estimate=pl.CostEstimate(flops=1 << 30, bytes_accessed=6 << 20, transcendentals=0),
    )(*[a.reshape(1024, 512) for a in (inputs, pre_act, cotangent)], mix_weight)
    depth, direct, mix = lax.optimization_barrier((exchange(depth, "py"), direct, mix))
    along_second = call(
        second_kernel, struct(512, 128), (depth, column(second_forward()), column(second_real()))
    )
    along_second = exchange(along_second.reshape(16, 32, 128), "px").reshape(512, 128)
    along_first = call(
        first_kernel,
        struct(256, 128),
        (along_second, jnp.asarray(first_twiddle()), column(first_halves()), mix),
    )
    spectra = exchange(along_first.reshape(16, 16, 128), "py").reshape(256, 128)
    mode_back, xr, xi, b1, mix = call(
        mode_kernel,
        (struct(64, 128), struct(64, 128), struct(64, 128), struct(32, 128), struct(2, 128)),
        (spectra, spectral_weight.reshape(2048, 128)),
    )
    mode_back = exchange(mode_back.reshape(16, 4, 128), "py").reshape(64, 128)
    spectral_grad = call(
        outer_kernel,
        struct(2048, 128),
        (xr, xi, b1),
        8,
        pl.CostEstimate(flops=1 << 20, bytes_accessed=1 << 20, transcendentals=0),
    ).reshape(spectral_weight.shape)
    first_high, first_low = pair(first_inverse())
    first_table = np.concatenate([first_high, first_low, first_high], axis=0)
    first_back = call(
        first_back_kernel, struct(288, 128), (mode_back, jnp.asarray(first_table), mix)
    )
    first_back = exchange(first_back.reshape(16, 1, 2304), "px").reshape(288, 128)
    second_back = call(
        second_back_kernel,
        struct(16, 128, 128),
        (first_back, jnp.asarray(stacked(second_inverse()))),
    )
    gathered = exchange(second_back, "py")
    input_grad, mix_grad = pl.pallas_call(
        end_kernel,
        out_shape=(struct(4, N, N, 512), struct(C, C)),
        in_specs=whole(1) + [anywhere] * 2,
        out_specs=(anywhere, anywhere),
        scratch_shapes=[
            field,
            pltpu.VMEM((512, 512), BF16),
            field,
            pltpu.VMEM((C, C), F32),
            pltpu.SemaphoreType.DMA((2,)),
            pltpu.SemaphoreType.DMA((PARTS,)),
            pltpu.SemaphoreType.DMA((PARTS,)),
        ],
        compiler_params=params(20),
    )(gathered, direct.reshape(4, N, N, 512), column(depth_inverse()))
    return (input_grad.reshape(inputs.shape), spectral_grad, mix_grad)


def solution(mesh):
    placed = (
        P(None, "px", "py"),
        P(None, "px", "py"),
        P(None, "px", "py"),
        P(),
        P("py", "px", None, None, None),
    )
    return jax.shard_map(
        per_device,
        mesh=mesh,
        in_specs=placed,
        out_specs=(P(None, "px", "py"), P("py", "px", None, None, None), P()),
        check_vma=False,
    )
```

```python
import math

import jax
import jax.numpy as jnp
import ml_dtypes
import numpy as np
from jax import lax
from jax.experimental import pallas as pl
from jax.experimental.pallas import tpu as pltpu
from jax.sharding import PartitionSpec as P

C = 64
NX = 256
NY = 256
NZ = 32
MZ = 8
CELLS = NX * NY * NZ
N = 16
ROWS = 240
HALF = ROWS // 2
PER = 4
PARTS = N // PER
F32 = jnp.float32
BF16 = jnp.bfloat16


def pair(table):
    high = table.astype(ml_dtypes.bfloat16)
    low = (table - high.astype(np.float64)).astype(high.dtype)
    return high, low


def column(table):
    return jnp.asarray(np.concatenate(pair(table), axis=0))


def frequency(index):
    return np.where(index < 16, index, index - 32)


def angle(a, b, length):
    return 2.0 * np.pi / length * np.mod(a * b, length)


def depth_parts(cells):
    k, z = np.arange(8)[:, None], np.arange(32)[None, :]
    t = angle(k, z, 32)
    parts = np.stack([np.cos(t), -np.sin(t)], 1)
    return np.einsum("krz,ab->krabz", parts, np.eye(cells)).reshape(8, 2, cells, cells * 32)


def depth_sent():
    return np.delete(depth_parts(8).reshape(128, 256), np.arange(8, 16), axis=0)


def depth_inverse():
    return depth_parts(8).reshape(4, 2, 16, 256).transpose(1, 0, 2, 3).reshape(128, 256)


def second_forward():
    q = np.arange(32)
    t = angle(frequency(q)[:, None], np.arange(256)[None, :], 256)
    c, s = np.cos(t), np.sin(t)
    full = np.stack([np.stack([c, s], 1), np.stack([-s, c], 1)], 0)
    full = full.reshape(2, 16, 2, 2, 16, 2, 8)
    return full.transpose(0, 2, 1, 4, 5, 3, 6).reshape(64, 512)


def second_real():
    return second_forward().reshape(64, 32, 2, 8)[:, :, 0].reshape(64, 256)


def second_inverse():
    q = np.arange(32)
    t = angle(frequency(q)[:, None], np.arange(256)[None, :], 256)
    c, s = np.cos(t), np.sin(t)
    full = np.stack([np.stack([c, s], 0), np.stack([-s, c], 0)], 0)
    full = full.reshape(2, 2, 16, 2, 16, 2, 8)
    return full.transpose(4, 5, 1, 6, 0, 3, 2).reshape(512, 64)


def first_twiddle():
    t = angle(np.arange(16)[:, None], np.arange(128)[None, :] % 16, 256)
    return np.concatenate([np.cos(t), np.sin(t)], 0).astype(np.float32)


def first_halves():
    t = angle(np.arange(2)[:, None], np.arange(16)[None, :], 16)
    c, s = np.cos(t), np.sin(t)
    full = np.stack([np.stack([c, -s], 1), np.stack([s, c], 1)], 1)
    return np.einsum("hsrx,ab->hsarbx", full, np.eye(8)).reshape(32, 256)


def first_inverse():
    p = np.arange(32)
    t = angle(frequency(p)[:, None], np.arange(256)[None, :], 256)
    full = np.stack([np.cos(t), np.sin(t)], 0).reshape(2, 16, 2, 256)
    return full.transpose(0, 2, 1, 3).reshape(64, 256)


def split(values):
    high = values.astype(BF16)
    low = (values - high.astype(F32)).astype(BF16)
    return high, low


def dot(a, b, dims=((1,), (0,))):
    return lax.dot_general(a, b, (dims, ((), ())), preferred_element_type=F32)


def dot3(a, b, dims=((1,), (0,))):
    return dot(a[0], b[0], dims) + (dot(a[0], b[1], dims) + dot(a[1], b[0], dims))


def lanes(shape):
    return lax.broadcasted_iota(jnp.int32, shape, len(shape) - 1)


def transpose_groups(blocks, width):
    blocks = list(blocks)
    count = len(blocks)
    group = lanes(blocks[0].shape) // width
    step = 1
    while step < count:
        upper = (group & step) != 0
        for i in range(count):
            if i & step:
                continue
            a, b = blocks[i], blocks[i | step]
            blocks[i] = jnp.where(upper, pltpu.roll(b, step * width, 1), a)
            blocks[i | step] = jnp.where(upper, b, pltpu.roll(a, 128 - step * width, 1))
        step *= 2
    return blocks


def fft(parts):
    count = len(parts)
    if count == 1:
        return parts
    even, odd = fft(parts[0::2]), fft(parts[1::2])
    out = [None] * count
    for j in range(count // 2):
        er, ei = even[j]
        orr, oi = odd[j]
        if j == 0:
            tr, ti = orr, oi
        elif 4 * j == count:
            tr, ti = oi, -orr
        else:
            c, s = math.cos(2 * math.pi * j / count), math.sin(2 * math.pi * j / count)
            tr, ti = orr * c + oi * s, oi * c - orr * s
        out[j] = (er + tr, ei + ti)
        out[j + count // 2] = (er - tr, ei - ti)
    return out


def slope(v):
    cumulative = 0.5 * (1.0 + lax.erf(v * (1.0 / math.sqrt(2.0))))
    density = jnp.exp(-0.5 * v * v) * (1.0 / math.sqrt(2.0 * math.pi))
    return cumulative + v * density


def start_kernel(x_hbm, pre_hbm, cot_hbm, table_ref, out_hbm, x, pre, cot, out, in_sems, out_sems):
    moves = []
    for i in range(PARTS):
        at = pl.ds(PER * i, PER)
        three = [
            pltpu.make_async_copy(a.at[:, at], b.at[:, at], in_sems.at[n, i])
            for n, (a, b) in enumerate([(pre_hbm, pre), (cot_hbm, cot), (x_hbm, x)])
        ]
        for move in three:
            move.start()
        moves.append(three)
    both = table_ref[...]
    sends = []
    for i in range(PARTS):
        for move in moves[i]:
            move.wait()
        own = slice(PER * i, PER * i + PER)
        grad = cot[:, own] * slope(pre[:, own])
        for j in range(0, PER, 2):
            rows = []
            for n in (j, j + 1):
                rows += [x[c, PER * i + n] for c in range(4)] + [grad[c, n] for c in range(4)]
            rows = jnp.concatenate(rows, axis=0)
            for half in range(2):
                high, low = split(rows[:, 256 * half : 256 * half + 256])
                two = dot(both, high, ((1,), (1,)))
                done = two[:HALF] + (two[HALF:] + dot(both[:HALF], low, ((1,), (1,))))
                for n in range(2):
                    at = slice(HALF * half, HALF * half + HALF)
                    out[PER * i + j + n, at] = done[:, 128 * n : 128 * n + 128]
        at = pl.ds(PER * i, PER)
        send = pltpu.make_async_copy(out.at[at], out_hbm.at[at], out_sems.at[i])
        send.start()
        sends.append(send)
    for send in sends:
        send.wait()


def second_kernel(in_ref, table_ref, real_ref, out_ref):
    for k in range(8):
        at, size = (0, 8) if k == 0 else (16 * k - 8, 16)
        both = real_ref[...] if k == 0 else table_ref[...]
        pieces = [(s, at + HALF * half) for s in range(16) for half in range(2)]
        rows = jnp.concatenate([in_ref[s, a : a + size, :] for s, a in pieces], axis=0)
        high, low = split(rows)
        two = dot(both, high)
        done = two[:64] + (two[64:] + dot(both[:64], low))
        for ri in range(2):
            for q in range(2):
                j = 2 * ri + q
                out_ref[pl.ds(ri * 16 + k * 2 + q, 16, stride=32), :] = done[16 * j : 16 * j + 16]


def first_kernel(in_ref, tw_ref, table_ref, mix_ref, out_ref):
    parts = [(in_ref[32 * s : 32 * s + 16], in_ref[32 * s + 16 : 32 * s + 32]) for s in range(16)]
    rows = []
    for r, (re, im) in enumerate(fft(parts)):
        c, s = tw_ref[r : r + 1], tw_ref[16 + r : 17 + r]
        rows.append(jnp.concatenate([re * c + im * s, im * c - re * s], axis=1))
    data = split(jnp.concatenate(rows, axis=0))
    done = dot3((table_ref[:32], table_ref[32:]), data, ((1,), (1,)))
    for h in range(2):
        for b in range(8):
            tile = done[16 * h : 16 * h + 16, 128 * (b // 4) : 128 * (b // 4) + 128]
            if b % 4:
                tile = pltpu.roll(tile, 128 - 32 * (b % 4), 1)
            d = 8 * h + b
            out_ref[16 * d : 16 * d + 16] = tile
            out_ref[16 * d : 16 * d + 4, 64:128] = mix_ref[4 * d : 4 * d + 4, 64:128]


def swap_halves(b1):
    turned = pltpu.roll(b1, 64, 1)
    return jnp.where(lanes(b1.shape) < 64, turned, -turned)


def mode_kernel(in_ref, w_ref, out_ref, xr_ref, xi_ref, b1_ref, mix_ref):
    def field(ri, f):
        return jnp.concatenate(
            [in_ref[pl.ds(8 * ri + 4 * f + c, 16, stride=16), :] for c in range(4)], axis=0
        )

    spread = jnp.concatenate([field(0, 1), field(1, 1)], axis=0).T[:32]
    mode = lax.broadcasted_iota(jnp.int32, (32, 128), 0)
    b1 = spread * jnp.where((mode // 2) % 8 == 0, 1.0 / CELLS, 2.0 / CELLS)
    b2 = swap_halves(b1)
    lane = lanes((64, 128))
    total = jnp.zeros((64, 128), F32)
    for m in range(32):
        p, k, q = m // 16, (m // 2) % 8, m % 2
        at = ((p * 2 + q) * 8 + k) * 64
        weight = w_ref[at : at + 64]
        place = q + 4 * (k // 2) + 16 * p + 64 * (k % 2)
        real = jnp.sum(weight * b1[m : m + 1], axis=1, keepdims=True)
        imag = jnp.sum(weight * b2[m : m + 1], axis=1, keepdims=True)
        total = jnp.where(lane == place, real, total)
        total = jnp.where(lane == place + 2, imag, total)
    for c in range(4):
        out_ref[pl.ds(c, 16, stride=4), :] = total[16 * c : 16 * c + 16]
    xr_ref[...] = field(0, 0)
    xi_ref[...] = field(1, 0)
    b1_ref[...] = b1
    mix = in_ref[0:4]
    for s in range(1, 16):
        mix = mix + in_ref[16 * s : 16 * s + 4]
    mix_ref[...] = jnp.where(lanes((2, 128)) < 64, pltpu.roll(mix, 64, 1)[:2], mix[2:])


def outer_kernel(xr_ref, xi_ref, b1_ref, out_ref):
    xr, xi, b1 = xr_ref[...], xi_ref[...], b1_ref[...]
    b2 = swap_halves(b1)
    for m in range(32):
        p, k, q = m // 16, (m // 2) % 8, m % 2
        at = ((p * 2 + q) * 8 + k) * 64
        out_ref[at : at + 64] = xr[:, m : m + 1] * b1[m : m + 1] + xi[:, m : m + 1] * b2[m : m + 1]


def first_back_kernel(in_ref, t_ref, mix_ref, out_ref):
    parts = [in_ref[pl.ds(c, 16, stride=4), :] for c in range(4)]
    lane = lanes((16, 128))
    rows = []
    for p in range(2):
        merged = None
        for c in range(4):
            shift = (16 * (c - p)) % 128
            moved = pltpu.roll(parts[c], shift, 1) if shift else parts[c]
            merged = moved if merged is None else jnp.where((lane // 16) % 4 == c, moved, merged)
        rows.append(merged)
    re = jnp.concatenate(rows, axis=0)
    turned = jnp.where(
        (lanes((32, 128)) // 2) % 2 == 0, -pltpu.roll(re, 126, 1), pltpu.roll(re, 2, 1)
    )
    high, low = split(jnp.concatenate([re, turned], axis=0))
    done = dot(jnp.concatenate([high, high, low], axis=0), t_ref[...], ((0,), (0,)))
    mix = mix_ref[...]
    for t in range(2):
        blocks = [done[16 * b : 16 * b + 16, 128 * t : 128 * t + 128] for b in range(8)]
        for g, block in enumerate(transpose_groups(blocks, 16)):
            at = 18 * (8 * t + g)
            out_ref[at : at + 16] = block
            out_ref[at + 16 : at + 18] = mix


def second_back_kernel(in_ref, t_ref, out_ref):
    for k in range(4):
        rows = jnp.concatenate(
            [in_ref[pl.ds(4 * k + j, 16, stride=18), :] for j in range(4)], axis=0
        )
        high, low = split(rows)
        done = dot(t_ref[...], jnp.concatenate([high, high, low], axis=0))
        for y in range(16):
            for half in range(2):
                at, place = 32 * y + 16 * half, 64 * half + 16 * k
                out_ref[y, place : place + 16, :] = done[at : at + 16]
    mix = in_ref[16:18]
    for s in range(1, 16):
        mix = mix + in_ref[18 * s + 16 : 18 * s + 18]
    mix = jnp.concatenate([mix, pltpu.roll(mix, 64, 1)], axis=0)
    for y in range(16):
        out_ref[y, 8:12, 0:64] = mix[:, :64]


def end_kernel(
    in_ref, direct_hbm, table_hbm, out_hbm, mix_hbm, direct, table, out, mix, sems, in_sems, out_sems
):
    table_move = pltpu.make_async_copy(table_hbm, table, sems.at[0])
    table_move.start()
    moves = []
    for i in range(PARTS):
        at = pl.ds(PER * i, PER)
        move = pltpu.make_async_copy(direct_hbm.at[:, at], direct.at[:, at], in_sems.at[i])
        move.start()
        moves.append(move)
    for d in range(16):
        mix[4 * d : 4 * d + 4] = in_ref[d, 8:12, 0:64] * (1.0 / math.sqrt(CELLS))
    mix_move = pltpu.make_async_copy(mix, mix_hbm, sems.at[1])
    mix_move.start()
    sends = []
    for i in range(PARTS):
        rows = [[], []]
        for j in range(PER):
            turned = in_ref[PER * i + j].T
            for half in range(2):
                at = slice(64 * half, 64 * half + 64)
                rows[half].append(jnp.concatenate([turned[:64, at], turned[64:, at]], axis=1))
        if i == 0:
            table_move.wait()
        parts = []
        for half in range(2):
            high, low = split(jnp.concatenate(rows[half], axis=0))
            parts.append(
                dot(jnp.concatenate([high, high], axis=1), table[...]) + dot(low, table[:128])
            )
        done = jnp.concatenate(parts, axis=1)
        moves[i].wait()
        for j in range(PER):
            for c in range(4):
                at = 64 * j + 16 * c
                out[c, PER * i + j] = direct[c, PER * i + j] + done[at : at + 16]
        at = pl.ds(PER * i, PER)
        send = pltpu.make_async_copy(out.at[:, at], out_hbm.at[:, at], out_sems.at[i])
        send.start()
        sends.append(send)
    for send in sends:
        send.wait()
    mix_move.wait()


def side_kernel(x_ref, pre_ref, cot_ref, weight_ref, direct_ref, mix_ref):
    high, low = split(weight_ref[...])
    weight = jnp.concatenate([high, low, high], axis=1)
    total = jnp.zeros((64, 64), F32)
    for x in range(16):
        field = split(x_ref[pl.ds(x, 64, stride=16), :])
        at = pl.ds(x, 64, stride=16)
        gh, gl = split(cot_ref[at, :] * slope(pre_ref[at, :]))
        total = total + dot3(field, (gh, gl), ((1,), (1,)))
        direct_ref[pl.ds(x, 64, stride=16), :] = dot(weight, jnp.concatenate([gh, gh, gl], axis=0))
    total = jnp.concatenate([total, total], axis=1)
    first = pl.program_id(0) == 0

    @pl.when(first)
    def _():
        mix_ref[...] = total

    @pl.when(jnp.logical_not(first))
    def _():
        mix_ref[...] += total


def params(mebibytes):
    return pltpu.CompilerParams(vmem_limit_bytes=mebibytes << 20)


def whole(count):
    return [pl.BlockSpec(memory_space=pltpu.VMEM)] * count


def struct(*shape):
    return jax.ShapeDtypeStruct(shape, F32)


def call(body, outs, args, mebibytes=12, cost=None):
    many = isinstance(outs, tuple)
    return pl.pallas_call(
        body,
        out_shape=outs,
        in_specs=whole(len(args)),
        out_specs=tuple(whole(len(outs))) if many else whole(1)[0],
        compiler_params=params(mebibytes),
        cost_estimate=cost,
    )(*args)


def exchange(values, axis):
    return lax.all_to_all(values, axis, split_axis=0, concat_axis=0, tiled=True)


def stacked(table):
    high, low = pair(table)
    return np.concatenate([high, low, high], axis=1)


def per_device(inputs, pre_act, cotangent, mix_weight, spectral_weight):
    anywhere = pl.BlockSpec(memory_space=pltpu.HBM)
    field = pltpu.VMEM((4, N, N, 512), F32)
    shaped = [a.reshape(4, N, N, 512) for a in (inputs, pre_act, cotangent)]
    depth = pl.pallas_call(
        start_kernel,
        out_shape=struct(N, ROWS, 128),
        in_specs=[anywhere] * 3 + whole(1),
        out_specs=anywhere,
        scratch_shapes=[
            field,
            field,
            field,
            pltpu.VMEM((N, ROWS, 128), F32),
            pltpu.SemaphoreType.DMA((3, PARTS)),
            pltpu.SemaphoreType.DMA((PARTS,)),
        ],
        compiler_params=params(60),
    )(*shaped, column(depth_sent()))

    tile_spec = pl.BlockSpec((1024, 128), lambda i: (0, i))
    direct, mix = pl.pallas_call(
        side_kernel,
        grid=(4,),
        out_shape=(struct(1024, 512), struct(64, 128)),
        in_specs=[tile_spec] * 3 + [pl.BlockSpec((64, 64), lambda i: (0, 0))],
        out_specs=(tile_spec, pl.BlockSpec((64, 128), lambda i: (0, 0))),
        compiler_params=params(60),
        cost_estimate=pl.CostEstimate(flops=1 << 30, bytes_accessed=6 << 20, transcendentals=0),
    )(*[a.reshape(1024, 512) for a in (inputs, pre_act, cotangent)], mix_weight)
    depth, direct, mix = lax.optimization_barrier((exchange(depth, "py"), direct, mix))
    along_second = call(
        second_kernel, struct(512, 128), (depth, column(second_forward()), column(second_real()))
    )
    along_second = exchange(along_second.reshape(16, 32, 128), "px").reshape(512, 128)
    along_first = call(
        first_kernel,
        struct(256, 128),
        (along_second, jnp.asarray(first_twiddle()), column(first_halves()), mix),
    )
    spectra = exchange(along_first.reshape(16, 16, 128), "py").reshape(256, 128)
    mode_back, xr, xi, b1, mix = call(
        mode_kernel,
        (struct(64, 128), struct(64, 128), struct(64, 128), struct(32, 128), struct(2, 128)),
        (spectra, spectral_weight.reshape(2048, 128)),
    )
    mode_back = exchange(mode_back.reshape(16, 4, 128), "py").reshape(64, 128)
    spectral_grad = call(
        outer_kernel,
        struct(2048, 128),
        (xr, xi, b1),
        8,
        pl.CostEstimate(flops=1 << 20, bytes_accessed=1 << 20, transcendentals=0),
    ).reshape(spectral_weight.shape)
    first_high, first_low = pair(first_inverse())
    first_table = np.concatenate([first_high, first_low, first_high], axis=0)
    first_back = call(
        first_back_kernel, struct(288, 128), (mode_back, jnp.asarray(first_table), mix)
    )
    first_back = exchange(first_back.reshape(16, 1, 2304), "px").reshape(288, 128)
    second_back = call(
        second_back_kernel,
        struct(16, 128, 128),
        (first_back, jnp.asarray(stacked(second_inverse()))),
    )
    gathered = exchange(second_back, "py")
    input_grad, mix_grad = pl.pallas_call(
        end_kernel,
        out_shape=(struct(4, N, N, 512), struct(C, C)),
        in_specs=whole(1) + [anywhere] * 2,
        out_specs=(anywhere, anywhere),
        scratch_shapes=[
            field,
            pltpu.VMEM((256, 256), BF16),
            field,
            pltpu.VMEM((C, C), F32),
            pltpu.SemaphoreType.DMA((2,)),
            pltpu.SemaphoreType.DMA((PARTS,)),
            pltpu.SemaphoreType.DMA((PARTS,)),
        ],
        compiler_params=params(20),
    )(gathered, direct.reshape(4, N, N, 512), column(depth_inverse()))
    return (input_grad.reshape(inputs.shape), spectral_grad, mix_grad)


def solution(mesh):
    placed = (
        P(None, "px", "py"),
        P(None, "px", "py"),
        P(None, "px", "py"),
        P(),
        P("py", "px", None, None, None),
    )
    return jax.shard_map(
        per_device,
        mesh=mesh,
        in_specs=placed,
        out_specs=(P(None, "px", "py"), P("py", "px", None, None, None), P()),
        check_vma=False,
    )
```

```python
import math

import jax
import jax.numpy as jnp
import ml_dtypes
import numpy as np
from jax import lax
from jax.experimental import pallas as pl
from jax.experimental.pallas import tpu as pltpu
from jax.sharding import PartitionSpec as P

C = 64
NX = 256
NY = 256
NZ = 32
MZ = 8
CELLS = NX * NY * NZ
N = 16
ROWS = 240
HALF = ROWS // 2
START_PARTS = (4, 4, 4, 4)
END_PARTS = (4, 4, 4, 4)
F32 = jnp.float32
BF16 = jnp.bfloat16


def pair(table):
    high = table.astype(ml_dtypes.bfloat16)
    low = (table - high.astype(np.float64)).astype(high.dtype)
    return high, low


def column(table):
    return jnp.asarray(np.concatenate(pair(table), axis=0))


def frequency(index):
    return np.where(index < 16, index, index - 32)


def angle(a, b, length):
    return 2.0 * np.pi / length * np.mod(a * b, length)


def depth_parts(cells):
    k, z = np.arange(8)[:, None], np.arange(32)[None, :]
    t = angle(k, z, 32)
    parts = np.stack([np.cos(t), -np.sin(t)], 1)
    return np.einsum("krz,ab->krabz", parts, np.eye(cells)).reshape(8, 2, cells, cells * 32)


def depth_sent():
    return np.delete(depth_parts(8).reshape(128, 256), np.arange(8, 16), axis=0)


def depth_inverse():
    return depth_parts(8).reshape(4, 2, 16, 256).transpose(1, 0, 2, 3).reshape(128, 256)


def second_forward():
    q = np.arange(32)
    t = angle(frequency(q)[:, None], np.arange(256)[None, :], 256)
    c, s = np.cos(t), np.sin(t)
    full = np.stack([np.stack([c, s], 1), np.stack([-s, c], 1)], 0)
    full = full.reshape(2, 16, 2, 2, 16, 2, 8)
    return full.transpose(0, 2, 1, 4, 5, 3, 6).reshape(64, 512)


def second_real():
    return second_forward().reshape(64, 32, 2, 8)[:, :, 0].reshape(64, 256)


def second_inverse():
    q = np.arange(32)
    t = angle(frequency(q)[:, None], np.arange(256)[None, :], 256)
    c, s = np.cos(t), np.sin(t)
    full = np.stack([np.stack([c, s], 0), np.stack([-s, c], 0)], 0)
    full = full.reshape(2, 2, 16, 2, 16, 2, 8)
    return full.transpose(4, 5, 1, 6, 0, 3, 2).reshape(512, 64)


def first_twiddle():
    t = angle(np.arange(16)[:, None], np.arange(128)[None, :] % 16, 256)
    return np.concatenate([np.cos(t), np.sin(t)], 0).astype(np.float32)


def first_halves():
    t = angle(np.arange(2)[:, None], np.arange(16)[None, :], 16)
    c, s = np.cos(t), np.sin(t)
    full = np.stack([np.stack([c, -s], 1), np.stack([s, c], 1)], 1)
    return np.einsum("hsrx,ab->hsarbx", full, np.eye(8)).reshape(32, 256)


def first_inverse():
    p = np.arange(32)
    t = angle(frequency(p)[:, None], np.arange(256)[None, :], 256)
    full = np.stack([np.cos(t), np.sin(t)], 0).reshape(2, 16, 2, 256)
    return full.transpose(0, 2, 1, 3).reshape(64, 256)


def spans(sizes):
    return [(sum(sizes[:i]), size) for i, size in enumerate(sizes)]


def split(values):
    high = values.astype(BF16)
    low = (values - high.astype(F32)).astype(BF16)
    return high, low


def dot(a, b, dims=((1,), (0,))):
    return lax.dot_general(a, b, (dims, ((), ())), preferred_element_type=F32)


def dot3(a, b, dims=((1,), (0,))):
    return dot(a[0], b[0], dims) + (dot(a[0], b[1], dims) + dot(a[1], b[0], dims))


def lanes(shape):
    return lax.broadcasted_iota(jnp.int32, shape, len(shape) - 1)


def transpose_groups(blocks, width):
    blocks = list(blocks)
    count = len(blocks)
    group = lanes(blocks[0].shape) // width
    step = 1
    while step < count:
        upper = (group & step) != 0
        for i in range(count):
            if i & step:
                continue
            a, b = blocks[i], blocks[i | step]
            blocks[i] = jnp.where(upper, pltpu.roll(b, step * width, 1), a)
            blocks[i | step] = jnp.where(upper, b, pltpu.roll(a, 128 - step * width, 1))
        step *= 2
    return blocks


def fft(parts):
    count = len(parts)
    if count == 1:
        return parts
    even, odd = fft(parts[0::2]), fft(parts[1::2])
    out = [None] * count
    for j in range(count // 2):
        er, ei = even[j]
        orr, oi = odd[j]
        if j == 0:
            tr, ti = orr, oi
        elif 4 * j == count:
            tr, ti = oi, -orr
        else:
            c, s = math.cos(2 * math.pi * j / count), math.sin(2 * math.pi * j / count)
            tr, ti = orr * c + oi * s, oi * c - orr * s
        out[j] = (er + tr, ei + ti)
        out[j + count // 2] = (er - tr, ei - ti)
    return out


def slope(v):
    cumulative = 0.5 * (1.0 + lax.erf(v * (1.0 / math.sqrt(2.0))))
    density = jnp.exp(-0.5 * v * v) * (1.0 / math.sqrt(2.0 * math.pi))
    return cumulative + v * density


def start_kernel(x_hbm, pre_hbm, cot_hbm, table_ref, out_hbm, x, pre, cot, out, in_sems, out_sems):
    moves = []
    for i, (first, size) in enumerate(spans(START_PARTS)):
        at = pl.ds(first, size)
        three = [
            pltpu.make_async_copy(a.at[:, at], b.at[:, at], in_sems.at[n, i])
            for n, (a, b) in enumerate([(pre_hbm, pre), (cot_hbm, cot), (x_hbm, x)])
        ]
        for move in three:
            move.start()
        moves.append(three)
    both = table_ref[...]
    sends = []
    for i, (first, size) in enumerate(spans(START_PARTS)):
        for move in moves[i]:
            move.wait()
        own = slice(first, first + size)
        grad = cot[:, own] * slope(pre[:, own])
        for j in range(0, size, 2):
            rows = []
            for n in (j, j + 1):
                rows += [x[c, first + n] for c in range(4)] + [grad[c, n] for c in range(4)]
            rows = jnp.concatenate(rows, axis=0)
            for half in range(2):
                high, low = split(rows[:, 256 * half : 256 * half + 256])
                two = dot(both, high, ((1,), (1,)))
                done = two[:HALF] + (two[HALF:] + dot(both[:HALF], low, ((1,), (1,))))
                for n in range(2):
                    at = slice(HALF * half, HALF * half + HALF)
                    out[first + j + n, at] = done[:, 128 * n : 128 * n + 128]
        at = pl.ds(first, size)
        send = pltpu.make_async_copy(out.at[at], out_hbm.at[at], out_sems.at[i])
        send.start()
        sends.append(send)
    for send in sends:
        send.wait()


def second_kernel(in_ref, table_ref, real_ref, out_ref):
    for k in range(8):
        at, size = (0, 8) if k == 0 else (16 * k - 8, 16)
        both = real_ref[...] if k == 0 else table_ref[...]
        pieces = [(s, at + HALF * half) for s in range(16) for half in range(2)]
        rows = jnp.concatenate([in_ref[s, a : a + size, :] for s, a in pieces], axis=0)
        high, low = split(rows)
        two = dot(both, high)
        done = two[:64] + (two[64:] + dot(both[:64], low))
        for ri in range(2):
            for q in range(2):
                j = 2 * ri + q
                out_ref[pl.ds(ri * 16 + k * 2 + q, 16, stride=32), :] = done[16 * j : 16 * j + 16]


def first_kernel(in_ref, tw_ref, table_ref, mix_ref, out_ref):
    parts = [(in_ref[32 * s : 32 * s + 16], in_ref[32 * s + 16 : 32 * s + 32]) for s in range(16)]
    rows = []
    for r, (re, im) in enumerate(fft(parts)):
        c, s = tw_ref[r : r + 1], tw_ref[16 + r : 17 + r]
        rows.append(jnp.concatenate([re * c + im * s, im * c - re * s], axis=1))
    data = split(jnp.concatenate(rows, axis=0))
    done = dot3((table_ref[:32], table_ref[32:]), data, ((1,), (1,)))
    for h in range(2):
        for b in range(8):
            tile = done[16 * h : 16 * h + 16, 128 * (b // 4) : 128 * (b // 4) + 128]
            if b % 4:
                tile = pltpu.roll(tile, 128 - 32 * (b % 4), 1)
            d = 8 * h + b
            out_ref[16 * d : 16 * d + 16] = tile
            out_ref[16 * d : 16 * d + 4, 64:128] = mix_ref[4 * d : 4 * d + 4, 64:128]


def swap_halves(b1):
    turned = pltpu.roll(b1, 64, 1)
    return jnp.where(lanes(b1.shape) < 64, turned, -turned)


def mode_kernel(in_ref, w_ref, out_ref, xr_ref, xi_ref, b1_ref, mix_ref):
    def field(ri, f):
        return jnp.concatenate(
            [in_ref[pl.ds(8 * ri + 4 * f + c, 16, stride=16), :] for c in range(4)], axis=0
        )

    spread = jnp.concatenate([field(0, 1), field(1, 1)], axis=0).T[:32]
    mode = lax.broadcasted_iota(jnp.int32, (32, 128), 0)
    b1 = spread * jnp.where((mode // 2) % 8 == 0, 1.0 / CELLS, 2.0 / CELLS)
    b2 = swap_halves(b1)
    lane = lanes((64, 128))
    total = jnp.zeros((64, 128), F32)
    for m in range(32):
        p, k, q = m // 16, (m // 2) % 8, m % 2
        at = ((p * 2 + q) * 8 + k) * 64
        weight = w_ref[at : at + 64]
        place = q + 4 * (k // 2) + 16 * p + 64 * (k % 2)
        real = jnp.sum(weight * b1[m : m + 1], axis=1, keepdims=True)
        imag = jnp.sum(weight * b2[m : m + 1], axis=1, keepdims=True)
        total = jnp.where(lane == place, real, total)
        total = jnp.where(lane == place + 2, imag, total)
    for c in range(4):
        out_ref[pl.ds(c, 16, stride=4), :] = total[16 * c : 16 * c + 16]
    xr_ref[...] = field(0, 0)
    xi_ref[...] = field(1, 0)
    b1_ref[...] = b1
    mix = in_ref[0:4]
    for s in range(1, 16):
        mix = mix + in_ref[16 * s : 16 * s + 4]
    mix_ref[...] = jnp.where(lanes((2, 128)) < 64, pltpu.roll(mix, 64, 1)[:2], mix[2:])


def outer_kernel(xr_ref, xi_ref, b1_ref, out_ref):
    xr, xi, b1 = xr_ref[...], xi_ref[...], b1_ref[...]
    b2 = swap_halves(b1)
    for m in range(32):
        p, k, q = m // 16, (m // 2) % 8, m % 2
        at = ((p * 2 + q) * 8 + k) * 64
        out_ref[at : at + 64] = xr[:, m : m + 1] * b1[m : m + 1] + xi[:, m : m + 1] * b2[m : m + 1]


def first_back_kernel(in_ref, t_ref, mix_ref, out_ref):
    parts = [in_ref[pl.ds(c, 16, stride=4), :] for c in range(4)]
    lane = lanes((16, 128))
    rows = []
    for p in range(2):
        merged = None
        for c in range(4):
            shift = (16 * (c - p)) % 128
            moved = pltpu.roll(parts[c], shift, 1) if shift else parts[c]
            merged = moved if merged is None else jnp.where((lane // 16) % 4 == c, moved, merged)
        rows.append(merged)
    re = jnp.concatenate(rows, axis=0)
    turned = jnp.where(
        (lanes((32, 128)) // 2) % 2 == 0, -pltpu.roll(re, 126, 1), pltpu.roll(re, 2, 1)
    )
    high, low = split(jnp.concatenate([re, turned], axis=0))
    done = dot(jnp.concatenate([high, high, low], axis=0), t_ref[...], ((0,), (0,)))
    mix = mix_ref[...]
    for t in range(2):
        blocks = [done[16 * b : 16 * b + 16, 128 * t : 128 * t + 128] for b in range(8)]
        for g, block in enumerate(transpose_groups(blocks, 16)):
            at = 18 * (8 * t + g)
            out_ref[at : at + 16] = block
            out_ref[at + 16 : at + 18] = mix


def second_back_kernel(in_ref, t_ref, out_ref):
    for k in range(4):
        rows = jnp.concatenate(
            [in_ref[pl.ds(4 * k + j, 16, stride=18), :] for j in range(4)], axis=0
        )
        high, low = split(rows)
        done = dot(t_ref[...], jnp.concatenate([high, high, low], axis=0))
        for y in range(16):
            for half in range(2):
                at, place = 32 * y + 16 * half, 64 * half + 16 * k
                out_ref[y, place : place + 16, :] = done[at : at + 16]
    mix = in_ref[16:18]
    for s in range(1, 16):
        mix = mix + in_ref[18 * s + 16 : 18 * s + 18]
    mix = jnp.concatenate([mix, pltpu.roll(mix, 64, 1)], axis=0)
    for y in range(16):
        out_ref[y, 8:12, 0:64] = mix[:, :64]


def end_kernel(in_ref, direct_ref, table_ref, out_hbm, mix_hbm, out, mix, mix_sem, out_sems):
    for d in range(16):
        mix[4 * d : 4 * d + 4] = in_ref[d, 8:12, 0:64] * (1.0 / math.sqrt(CELLS))
    mix_move = pltpu.make_async_copy(mix, mix_hbm, mix_sem)
    mix_move.start()
    sends = []
    for i, (first, size) in enumerate(spans(END_PARTS)):
        rows = [[], []]
        for j in range(size):
            turned = in_ref[first + j].T
            for half in range(2):
                at = slice(64 * half, 64 * half + 64)
                rows[half].append(jnp.concatenate([turned[:64, at], turned[64:, at]], axis=1))
        parts = []
        for half in range(2):
            high, low = split(jnp.concatenate(rows[half], axis=0))
            parts.append(
                dot(jnp.concatenate([high, high], axis=1), table_ref[...]) + dot(low, table_ref[:128])
            )
        done = jnp.concatenate(parts, axis=1)
        for j in range(size):
            for c in range(4):
                at = 64 * j + 16 * c
                out[c, first + j] = direct_ref[c, first + j] + done[at : at + 16]
        at = pl.ds(first, size)
        send = pltpu.make_async_copy(out.at[:, at], out_hbm.at[:, at], out_sems.at[i])
        send.start()
        sends.append(send)
    for send in sends:
        send.wait()
    mix_move.wait()


def side_kernel(x_ref, pre_ref, cot_ref, weight_ref, direct_ref, mix_ref):
    high, low = split(weight_ref[...])
    weight = jnp.concatenate([high, low, high], axis=1)
    total = jnp.zeros((64, 64), F32)
    for x in range(16):
        field = split(x_ref[pl.ds(x, 64, stride=16), :])
        at = pl.ds(x, 64, stride=16)
        gh, gl = split(cot_ref[at, :] * slope(pre_ref[at, :]))
        total = total + dot3(field, (gh, gl), ((1,), (1,)))
        direct_ref[pl.ds(x, 64, stride=16), :] = dot(weight, jnp.concatenate([gh, gh, gl], axis=0))
    total = jnp.concatenate([total, total], axis=1)
    first = pl.program_id(0) == 0

    @pl.when(first)
    def _():
        mix_ref[...] = total

    @pl.when(jnp.logical_not(first))
    def _():
        mix_ref[...] += total


def params(mebibytes):
    return pltpu.CompilerParams(vmem_limit_bytes=mebibytes << 20)


def whole(count):
    return [pl.BlockSpec(memory_space=pltpu.VMEM)] * count


def struct(*shape):
    return jax.ShapeDtypeStruct(shape, F32)


def call(body, outs, args, mebibytes=12, cost=None):
    many = isinstance(outs, tuple)
    return pl.pallas_call(
        body,
        out_shape=outs,
        in_specs=whole(len(args)),
        out_specs=tuple(whole(len(outs))) if many else whole(1)[0],
        compiler_params=params(mebibytes),
        cost_estimate=cost,
    )(*args)


def exchange(values, axis):
    return lax.all_to_all(values, axis, split_axis=0, concat_axis=0, tiled=True)


def stacked(table):
    high, low = pair(table)
    return np.concatenate([high, low, high], axis=1)


def per_device(inputs, pre_act, cotangent, mix_weight, spectral_weight):
    anywhere = pl.BlockSpec(memory_space=pltpu.HBM)
    field = pltpu.VMEM((4, N, N, 512), F32)
    shaped = [a.reshape(4, N, N, 512) for a in (inputs, pre_act, cotangent)]
    depth = pl.pallas_call(
        start_kernel,
        out_shape=struct(N, ROWS, 128),
        in_specs=[anywhere] * 3 + whole(1),
        out_specs=anywhere,
        scratch_shapes=[
            field,
            field,
            field,
            pltpu.VMEM((N, ROWS, 128), F32),
            pltpu.SemaphoreType.DMA((3, len(START_PARTS))),
            pltpu.SemaphoreType.DMA((len(START_PARTS),)),
        ],
        compiler_params=params(60),
    )(*shaped, column(depth_sent()))

    tile_spec = pl.BlockSpec((1024, 128), lambda i: (0, i))
    direct, mix = pl.pallas_call(
        side_kernel,
        grid=(4,),
        out_shape=(struct(1024, 512), struct(64, 128)),
        in_specs=[tile_spec] * 3 + [pl.BlockSpec((64, 64), lambda i: (0, 0))],
        out_specs=(tile_spec, pl.BlockSpec((64, 128), lambda i: (0, 0))),
        compiler_params=params(60),
        cost_estimate=pl.CostEstimate(flops=1 << 30, bytes_accessed=6 << 20, transcendentals=0),
    )(*[a.reshape(1024, 512) for a in (inputs, pre_act, cotangent)], mix_weight)
    depth, direct, mix = lax.optimization_barrier((exchange(depth, "py"), direct, mix))
    along_second = call(
        second_kernel, struct(512, 128), (depth, column(second_forward()), column(second_real()))
    )
    along_second = exchange(along_second.reshape(16, 32, 128), "px").reshape(512, 128)
    along_first = call(
        first_kernel,
        struct(256, 128),
        (along_second, jnp.asarray(first_twiddle()), column(first_halves()), mix),
    )
    spectra = exchange(along_first.reshape(16, 16, 128), "py").reshape(256, 128)
    mode_back, xr, xi, b1, mix = call(
        mode_kernel,
        (struct(64, 128), struct(64, 128), struct(64, 128), struct(32, 128), struct(2, 128)),
        (spectra, spectral_weight.reshape(2048, 128)),
    )
    mode_back = exchange(mode_back.reshape(16, 4, 128), "py").reshape(64, 128)
    spectral_grad = call(
        outer_kernel,
        struct(2048, 128),
        (xr, xi, b1),
        8,
        pl.CostEstimate(flops=1 << 20, bytes_accessed=1 << 20, transcendentals=0),
    ).reshape(spectral_weight.shape)
    first_high, first_low = pair(first_inverse())
    first_table = np.concatenate([first_high, first_low, first_high], axis=0)
    first_back = call(
        first_back_kernel, struct(288, 128), (mode_back, jnp.asarray(first_table), mix)
    )
    first_back = exchange(first_back.reshape(16, 1, 2304), "px").reshape(288, 128)
    first_back, spectral_grad = lax.optimization_barrier((first_back, spectral_grad))
    second_back = call(
        second_back_kernel,
        struct(16, 128, 128),
        (first_back, jnp.asarray(stacked(second_inverse()))),
    )
    gathered = exchange(second_back, "py")
    input_grad, mix_grad = pl.pallas_call(
        end_kernel,
        out_shape=(struct(4, N, N, 512), struct(C, C)),
        in_specs=whole(3),
        out_specs=(anywhere, anywhere),
        scratch_shapes=[
            field,
            pltpu.VMEM((C, C), F32),
            pltpu.SemaphoreType.DMA,
            pltpu.SemaphoreType.DMA((len(END_PARTS),)),
        ],
        compiler_params=params(20),
    )(gathered, direct.reshape(4, N, N, 512), column(depth_inverse()))
    return (input_grad.reshape(inputs.shape), spectral_grad, mix_grad)


def solution(mesh):
    placed = (
        P(None, "px", "py"),
        P(None, "px", "py"),
        P(None, "px", "py"),
        P(),
        P("py", "px", None, None, None),
    )
    return jax.shard_map(
        per_device,
        mesh=mesh,
        in_specs=placed,
        out_specs=(P(None, "px", "py"), P("py", "px", None, None, None), P()),
        check_vma=False,
    )
```

```python
import math

import jax
import jax.numpy as jnp
import ml_dtypes
import numpy as np
from jax import lax
from jax.experimental import pallas as pl
from jax.experimental.pallas import tpu as pltpu
from jax.sharding import PartitionSpec as P

C = 64
NX = 256
NY = 256
NZ = 32
MZ = 8
CELLS = NX * NY * NZ
N = 16
ROWS = 240
HALF = ROWS // 2
START_PARTS = (4, 4, 4, 4)
END_PARTS = (4, 4, 4, 4)
F32 = jnp.float32
BF16 = jnp.bfloat16


def pair(table):
    high = table.astype(ml_dtypes.bfloat16)
    low = (table - high.astype(np.float64)).astype(high.dtype)
    return high, low


def column(table):
    return jnp.asarray(np.concatenate(pair(table), axis=0))


def frequency(index):
    return np.where(index < 16, index, index - 32)


def angle(a, b, length):
    return 2.0 * np.pi / length * np.mod(a * b, length)


def depth_parts(cells):
    k, z = np.arange(8)[:, None], np.arange(32)[None, :]
    t = angle(k, z, 32)
    parts = np.stack([np.cos(t), -np.sin(t)], 1)
    return np.einsum("krz,ab->krabz", parts, np.eye(cells)).reshape(8, 2, cells, cells * 32)


def depth_sent():
    return np.delete(depth_parts(8).reshape(128, 256), np.arange(8, 16), axis=0)


def depth_inverse():
    return depth_parts(8).reshape(4, 2, 16, 256).transpose(1, 0, 2, 3).reshape(128, 256)


def second_forward():
    q = np.arange(32)
    t = angle(frequency(q)[:, None], np.arange(256)[None, :], 256)
    c, s = np.cos(t), np.sin(t)
    full = np.stack([np.stack([c, s], 1), np.stack([-s, c], 1)], 0)
    full = full.reshape(2, 16, 2, 2, 16, 2, 8)
    return full.transpose(0, 2, 1, 4, 5, 3, 6).reshape(64, 512)


def second_real():
    return second_forward().reshape(64, 32, 2, 8)[:, :, 0].reshape(64, 256)


def second_inverse():
    q = np.arange(32)
    t = angle(frequency(q)[:, None], np.arange(256)[None, :], 256)
    c, s = np.cos(t), np.sin(t)
    full = np.stack([np.stack([c, s], 0), np.stack([-s, c], 0)], 0)
    full = full.reshape(2, 2, 16, 2, 16, 2, 8)
    return full.transpose(4, 5, 1, 6, 0, 3, 2).reshape(512, 64)


def first_twiddle():
    t = angle(np.arange(16)[:, None], np.arange(128)[None, :] % 16, 256)
    return np.concatenate([np.cos(t), np.sin(t)], 0).astype(np.float32)


def first_halves():
    t = angle(np.arange(2)[:, None], np.arange(16)[None, :], 16)
    c, s = np.cos(t), np.sin(t)
    full = np.stack([np.stack([c, -s], 1), np.stack([s, c], 1)], 1)
    return np.einsum("hsrx,ab->hsarbx", full, np.eye(8)).reshape(32, 256)


def first_inverse():
    p = np.arange(32)
    t = angle(frequency(p)[:, None], np.arange(256)[None, :], 256)
    full = np.stack([np.cos(t), np.sin(t)], 0).reshape(2, 16, 2, 256)
    return full.transpose(0, 2, 1, 3).reshape(64, 256)


def spans(sizes):
    return [(sum(sizes[:i]), size) for i, size in enumerate(sizes)]


def split(values):
    high = values.astype(BF16)
    low = (values - high.astype(F32)).astype(BF16)
    return high, low


def dot(a, b, dims=((1,), (0,))):
    return lax.dot_general(a, b, (dims, ((), ())), preferred_element_type=F32)


def dot3(a, b, dims=((1,), (0,))):
    return dot(a[0], b[0], dims) + (dot(a[0], b[1], dims) + dot(a[1], b[0], dims))


def lanes(shape):
    return lax.broadcasted_iota(jnp.int32, shape, len(shape) - 1)


def transpose_groups(blocks, width):
    blocks = list(blocks)
    count = len(blocks)
    group = lanes(blocks[0].shape) // width
    step = 1
    while step < count:
        upper = (group & step) != 0
        for i in range(count):
            if i & step:
                continue
            a, b = blocks[i], blocks[i | step]
            blocks[i] = jnp.where(upper, pltpu.roll(b, step * width, 1), a)
            blocks[i | step] = jnp.where(upper, b, pltpu.roll(a, 128 - step * width, 1))
        step *= 2
    return blocks


def fft(parts):
    count = len(parts)
    if count == 1:
        return parts
    even, odd = fft(parts[0::2]), fft(parts[1::2])
    out = [None] * count
    for j in range(count // 2):
        er, ei = even[j]
        orr, oi = odd[j]
        if j == 0:
            tr, ti = orr, oi
        elif 4 * j == count:
            tr, ti = oi, -orr
        else:
            c, s = math.cos(2 * math.pi * j / count), math.sin(2 * math.pi * j / count)
            tr, ti = orr * c + oi * s, oi * c - orr * s
        out[j] = (er + tr, ei + ti)
        out[j + count // 2] = (er - tr, ei - ti)
    return out


def slope(v):
    cumulative = 0.5 * (1.0 + lax.erf(v * (1.0 / math.sqrt(2.0))))
    density = jnp.exp(-0.5 * v * v) * (1.0 / math.sqrt(2.0 * math.pi))
    return cumulative + v * density


def start_kernel(x_hbm, pre_hbm, cot_hbm, table_ref, out_hbm, x, pre, cot, out, in_sems, out_sems):
    moves = []
    for i, (first, size) in enumerate(spans(START_PARTS)):
        at = pl.ds(first, size)
        three = [
            pltpu.make_async_copy(a.at[:, at], b.at[:, at], in_sems.at[n, i])
            for n, (a, b) in enumerate([(pre_hbm, pre), (cot_hbm, cot), (x_hbm, x)])
        ]
        for move in three:
            move.start()
        moves.append(three)
    both = table_ref[...]
    sends = []
    for i, (first, size) in enumerate(spans(START_PARTS)):
        for move in moves[i]:
            move.wait()
        own = slice(first, first + size)
        grad = cot[:, own] * slope(pre[:, own])
        for j in range(0, size, 2):
            rows = []
            for n in (j, j + 1):
                rows += [x[c, first + n] for c in range(4)] + [grad[c, n] for c in range(4)]
            rows = jnp.concatenate(rows, axis=0)
            for half in range(2):
                high, low = split(rows[:, 256 * half : 256 * half + 256])
                two = dot(both, high, ((1,), (1,)))
                done = two[:HALF] + (two[HALF:] + dot(both[:HALF], low, ((1,), (1,))))
                for n in range(2):
                    at = slice(HALF * half, HALF * half + HALF)
                    out[first + j + n, at] = done[:, 128 * n : 128 * n + 128]
        at = pl.ds(first, size)
        send = pltpu.make_async_copy(out.at[at], out_hbm.at[at], out_sems.at[i])
        send.start()
        sends.append(send)
    for send in sends:
        send.wait()


def second_kernel(in_ref, table_ref, real_ref, out_ref):
    for k in range(8):
        at, size = (0, 8) if k == 0 else (16 * k - 8, 16)
        both = real_ref[...] if k == 0 else table_ref[...]
        pieces = [(s, at + HALF * half) for s in range(16) for half in range(2)]
        rows = jnp.concatenate([in_ref[s, a : a + size, :] for s, a in pieces], axis=0)
        high, low = split(rows)
        two = dot(both, high)
        done = two[:64] + (two[64:] + dot(both[:64], low))
        for ri in range(2):
            for q in range(2):
                j = 2 * ri + q
                out_ref[pl.ds(ri * 16 + k * 2 + q, 16, stride=32), :] = done[16 * j : 16 * j + 16]


def first_kernel(in_ref, tw_ref, table_ref, mix_ref, out_ref):
    parts = [(in_ref[32 * s : 32 * s + 16], in_ref[32 * s + 16 : 32 * s + 32]) for s in range(16)]
    rows = []
    for r, (re, im) in enumerate(fft(parts)):
        c, s = tw_ref[r : r + 1], tw_ref[16 + r : 17 + r]
        rows.append(jnp.concatenate([re * c + im * s, im * c - re * s], axis=1))
    data = split(jnp.concatenate(rows, axis=0))
    done = dot3((table_ref[:32], table_ref[32:]), data, ((1,), (1,)))
    lane = lanes((2, 128))
    for h in range(2):
        for t in range(2):
            tile = slice(128 * t, 128 * t + 128)
            blocks = [done[16 * h + 4 * g : 16 * h + 4 * g + 4, tile] for g in range(4)]
            for b, block in enumerate(transpose_groups(blocks, 32)):
                d = 8 * h + 4 * t + b
                out_ref[6 * d : 6 * d + 4] = block
                out_ref[6 * d + 4 : 6 * d + 6] = jnp.where(
                    lane < 64, mix_ref[4 * d : 4 * d + 2], mix_ref[4 * d + 2 : 4 * d + 4]
                )


def swap_halves(b1):
    turned = pltpu.roll(b1, 64, 1)
    return jnp.where(lanes(b1.shape) < 64, turned, -turned)


def mode_kernel(in_ref, w_ref, out_ref, fields_ref, b1_ref, mix_ref):
    fields = jnp.concatenate([in_ref[pl.ds(c, 16, stride=6), :] for c in range(4)], axis=0)
    fields_ref[...] = fields
    turned = jnp.concatenate([fields, fields], axis=0).T
    spread = jnp.where(lanes((32, 128)) < 64, turned[32:64], turned[96:])
    mode = lax.broadcasted_iota(jnp.int32, (32, 128), 0)
    b1 = spread * jnp.where((mode // 2) % 8 == 0, 1.0 / CELLS, 2.0 / CELLS)
    b2 = swap_halves(b1)
    lane = lanes((64, 128))
    total = jnp.zeros((64, 128), F32)
    for m in range(32):
        p, k, q = m // 16, (m // 2) % 8, m % 2
        at = ((p * 2 + q) * 8 + k) * 64
        weight = w_ref[at : at + 64]
        place = q + 4 * (k // 2) + 16 * p + 64 * (k % 2)
        real = jnp.sum(weight * b1[m : m + 1], axis=1, keepdims=True)
        imag = jnp.sum(weight * b2[m : m + 1], axis=1, keepdims=True)
        total = jnp.where(lane == place, real, total)
        total = jnp.where(lane == place + 2, imag, total)
    for c in range(4):
        out_ref[pl.ds(c, 16, stride=4), :] = total[16 * c : 16 * c + 16]
    b1_ref[...] = b1
    mix = in_ref[4:6]
    for s in range(1, 16):
        mix = mix + in_ref[6 * s + 4 : 6 * s + 6]
    mix_ref[...] = mix


def outer_kernel(fields_ref, b1_ref, out_ref):
    fields, b1 = fields_ref[...], b1_ref[...]
    b2 = swap_halves(b1)
    for m in range(32):
        p, k, q = m // 16, (m // 2) % 8, m % 2
        at = ((p * 2 + q) * 8 + k) * 64
        real, imag = fields[:, m : m + 1], fields[:, 64 + m : 65 + m]
        out_ref[at : at + 64] = real * b1[m : m + 1] + imag * b2[m : m + 1]


def first_back_kernel(in_ref, t_ref, mix_ref, out_ref):
    parts = [in_ref[pl.ds(c, 16, stride=4), :] for c in range(4)]
    lane = lanes((16, 128))
    rows = []
    for p in range(2):
        merged = None
        for c in range(4):
            shift = (16 * (c - p)) % 128
            moved = pltpu.roll(parts[c], shift, 1) if shift else parts[c]
            merged = moved if merged is None else jnp.where((lane // 16) % 4 == c, moved, merged)
        rows.append(merged)
    re = jnp.concatenate(rows, axis=0)
    turned = jnp.where(
        (lanes((32, 128)) // 2) % 2 == 0, -pltpu.roll(re, 126, 1), pltpu.roll(re, 2, 1)
    )
    high, low = split(jnp.concatenate([re, turned], axis=0))
    done = dot(jnp.concatenate([high, high, low], axis=0), t_ref[...], ((0,), (0,)))
    mix = mix_ref[...]
    for t in range(2):
        blocks = [done[16 * b : 16 * b + 16, 128 * t : 128 * t + 128] for b in range(8)]
        for g, block in enumerate(transpose_groups(blocks, 16)):
            at = 18 * (8 * t + g)
            out_ref[at : at + 16] = block
            out_ref[at + 16 : at + 18] = mix


def second_back_kernel(in_ref, t_ref, out_ref):
    for k in range(4):
        rows = jnp.concatenate(
            [in_ref[pl.ds(4 * k + j, 16, stride=18), :] for j in range(4)], axis=0
        )
        high, low = split(rows)
        done = dot(t_ref[...], jnp.concatenate([high, high, low], axis=0))
        for y in range(16):
            for half in range(2):
                at, place = 32 * y + 16 * half, 64 * half + 16 * k
                out_ref[y, place : place + 16, :] = done[at : at + 16]
    mix = in_ref[16:18]
    for s in range(1, 16):
        mix = mix + in_ref[18 * s + 16 : 18 * s + 18]
    mix = jnp.concatenate([mix, pltpu.roll(mix, 64, 1)], axis=0)
    for y in range(16):
        out_ref[y, 8:12, 0:64] = mix[:, :64]


def end_kernel(in_ref, direct_ref, table_ref, out_hbm, mix_hbm, out, mix, mix_sem, out_sems):
    for d in range(16):
        mix[4 * d : 4 * d + 4] = in_ref[d, 8:12, 0:64] * (1.0 / math.sqrt(CELLS))
    mix_move = pltpu.make_async_copy(mix, mix_hbm, mix_sem)
    mix_move.start()
    sends = []
    for i, (first, size) in enumerate(spans(END_PARTS)):
        rows = [[], []]
        for j in range(size):
            turned = in_ref[first + j].T
            for half in range(2):
                at = slice(64 * half, 64 * half + 64)
                rows[half].append(jnp.concatenate([turned[:64, at], turned[64:, at]], axis=1))
        parts = []
        for half in range(2):
            high, low = split(jnp.concatenate(rows[half], axis=0))
            parts.append(
                dot(jnp.concatenate([high, high], axis=1), table_ref[...]) + dot(low, table_ref[:128])
            )
        done = jnp.concatenate(parts, axis=1)
        for j in range(size):
            for c in range(4):
                at = 64 * j + 16 * c
                out[c, first + j] = direct_ref[c, first + j] + done[at : at + 16]
        at = pl.ds(first, size)
        send = pltpu.make_async_copy(out.at[:, at], out_hbm.at[:, at], out_sems.at[i])
        send.start()
        sends.append(send)
    for send in sends:
        send.wait()
    mix_move.wait()


def side_kernel(x_ref, pre_ref, cot_ref, weight_ref, direct_ref, mix_ref):
    high, low = split(weight_ref[...])
    weight = jnp.concatenate([high, low, high], axis=1)
    total = jnp.zeros((64, 64), F32)
    for x in range(16):
        field = split(x_ref[pl.ds(x, 64, stride=16), :])
        at = pl.ds(x, 64, stride=16)
        gh, gl = split(cot_ref[at, :] * slope(pre_ref[at, :]))
        total = total + dot3(field, (gh, gl), ((1,), (1,)))
        direct_ref[pl.ds(x, 64, stride=16), :] = dot(weight, jnp.concatenate([gh, gh, gl], axis=0))
    total = jnp.concatenate([total, total], axis=1)
    first = pl.program_id(0) == 0

    @pl.when(first)
    def _():
        mix_ref[...] = total

    @pl.when(jnp.logical_not(first))
    def _():
        mix_ref[...] += total


def params(mebibytes):
    return pltpu.CompilerParams(vmem_limit_bytes=mebibytes << 20)


def whole(count):
    return [pl.BlockSpec(memory_space=pltpu.VMEM)] * count


def struct(*shape):
    return jax.ShapeDtypeStruct(shape, F32)


def call(body, outs, args, mebibytes=12, cost=None):
    many = isinstance(outs, tuple)
    return pl.pallas_call(
        body,
        out_shape=outs,
        in_specs=whole(len(args)),
        out_specs=tuple(whole(len(outs))) if many else whole(1)[0],
        compiler_params=params(mebibytes),
        cost_estimate=cost,
    )(*args)


def exchange(values, axis):
    return lax.all_to_all(values, axis, split_axis=0, concat_axis=0, tiled=True)


def stacked(table):
    high, low = pair(table)
    return np.concatenate([high, low, high], axis=1)


def per_device(inputs, pre_act, cotangent, mix_weight, spectral_weight):
    anywhere = pl.BlockSpec(memory_space=pltpu.HBM)
    field = pltpu.VMEM((4, N, N, 512), F32)
    shaped = [a.reshape(4, N, N, 512) for a in (inputs, pre_act, cotangent)]
    depth = pl.pallas_call(
        start_kernel,
        out_shape=struct(N, ROWS, 128),
        in_specs=[anywhere] * 3 + whole(1),
        out_specs=anywhere,
        scratch_shapes=[
            field,
            field,
            field,
            pltpu.VMEM((N, ROWS, 128), F32),
            pltpu.SemaphoreType.DMA((3, len(START_PARTS))),
            pltpu.SemaphoreType.DMA((len(START_PARTS),)),
        ],
        compiler_params=params(60),
    )(*shaped, column(depth_sent()))

    tile_spec = pl.BlockSpec((1024, 128), lambda i: (0, i))
    direct, mix = pl.pallas_call(
        side_kernel,
        grid=(4,),
        out_shape=(struct(1024, 512), struct(64, 128)),
        in_specs=[tile_spec] * 3 + [pl.BlockSpec((64, 64), lambda i: (0, 0))],
        out_specs=(tile_spec, pl.BlockSpec((64, 128), lambda i: (0, 0))),
        compiler_params=params(60),
        cost_estimate=pl.CostEstimate(flops=1 << 30, bytes_accessed=6 << 20, transcendentals=0),
    )(*[a.reshape(1024, 512) for a in (inputs, pre_act, cotangent)], mix_weight)
    depth, direct, mix = lax.optimization_barrier((exchange(depth, "py"), direct, mix))
    along_second = call(
        second_kernel, struct(512, 128), (depth, column(second_forward()), column(second_real()))
    )
    along_second = exchange(along_second.reshape(16, 32, 128), "px").reshape(512, 128)
    along_first = call(
        first_kernel,
        struct(96, 128),
        (along_second, jnp.asarray(first_twiddle()), column(first_halves()), mix),
    )
    spectra = exchange(along_first.reshape(16, 1, 768), "py").reshape(96, 128)
    mode_back, fields, b1, mix = call(
        mode_kernel,
        (struct(64, 128), struct(64, 128), struct(32, 128), struct(2, 128)),
        (spectra, spectral_weight.reshape(2048, 128)),
    )
    mode_back = exchange(mode_back.reshape(16, 4, 128), "py").reshape(64, 128)
    spectral_grad = call(
        outer_kernel,
        struct(2048, 128),
        (fields, b1),
        8,
        pl.CostEstimate(flops=1 << 20, bytes_accessed=1 << 20, transcendentals=0),
    ).reshape(spectral_weight.shape)
    first_high, first_low = pair(first_inverse())
    first_table = np.concatenate([first_high, first_low, first_high], axis=0)
    first_back = call(
        first_back_kernel, struct(288, 128), (mode_back, jnp.asarray(first_table), mix)
    )
    first_back = exchange(first_back.reshape(16, 1, 2304), "px").reshape(288, 128)
    first_back, spectral_grad = lax.optimization_barrier((first_back, spectral_grad))
    second_back = call(
        second_back_kernel,
        struct(16, 128, 128),
        (first_back, jnp.asarray(stacked(second_inverse()))),
    )
    gathered = exchange(second_back, "py")
    input_grad, mix_grad = pl.pallas_call(
        end_kernel,
        out_shape=(struct(4, N, N, 512), struct(C, C)),
        in_specs=whole(3),
        out_specs=(anywhere, anywhere),
        scratch_shapes=[
            field,
            pltpu.VMEM((C, C), F32),
            pltpu.SemaphoreType.DMA,
            pltpu.SemaphoreType.DMA((len(END_PARTS),)),
        ],
        compiler_params=params(20),
    )(gathered, direct.reshape(4, N, N, 512), column(depth_inverse()))
    return (input_grad.reshape(inputs.shape), spectral_grad, mix_grad)


def solution(mesh):
    placed = (
        P(None, "px", "py"),
        P(None, "px", "py"),
        P(None, "px", "py"),
        P(),
        P("py", "px", None, None, None),
    )
    return jax.shard_map(
        per_device,
        mesh=mesh,
        in_specs=placed,
        out_specs=(P(None, "px", "py"), P("py", "px", None, None, None), P()),
        check_vma=False,
    )
```

```python
import math

import jax
import jax.numpy as jnp
import ml_dtypes
import numpy as np
from jax import lax
from jax.experimental import pallas as pl
from jax.experimental.pallas import tpu as pltpu
from jax.sharding import PartitionSpec as P

C = 64
NX = 256
NY = 256
NZ = 32
MZ = 8
CELLS = NX * NY * NZ
N = 16
ROWS = 240
HALF = ROWS // 2
START_PARTS = (4, 4, 4, 4)
END_PARTS = (4, 4, 4, 4)
F32 = jnp.float32
BF16 = jnp.bfloat16


def pair(table):
    high = table.astype(ml_dtypes.bfloat16)
    low = (table - high.astype(np.float64)).astype(high.dtype)
    return high, low


def column(table):
    return jnp.asarray(np.concatenate(pair(table), axis=0))


def frequency(index):
    return np.where(index < 16, index, index - 32)


def angle(a, b, length):
    return 2.0 * np.pi / length * np.mod(a * b, length)


def depth_parts(cells):
    k, z = np.arange(8)[:, None], np.arange(32)[None, :]
    t = angle(k, z, 32)
    parts = np.stack([np.cos(t), -np.sin(t)], 1)
    return np.einsum("krz,ab->krabz", parts, np.eye(cells)).reshape(8, 2, cells, cells * 32)


def depth_sent():
    return np.delete(depth_parts(8).reshape(128, 256), np.arange(8, 16), axis=0)


def depth_inverse():
    return depth_parts(8).reshape(4, 2, 16, 256).transpose(1, 0, 2, 3).reshape(128, 256)


def second_forward():
    q = np.arange(32)
    t = angle(frequency(q)[:, None], np.arange(256)[None, :], 256)
    c, s = np.cos(t), np.sin(t)
    full = np.stack([np.stack([c, s], 1), np.stack([-s, c], 1)], 0)
    full = full.reshape(2, 16, 2, 2, 16, 2, 8)
    return full.transpose(0, 2, 1, 4, 5, 3, 6).reshape(64, 512)


def second_real():
    return second_forward().reshape(64, 32, 2, 8)[:, :, 0].reshape(64, 256)


def second_inverse():
    q = np.arange(32)
    t = angle(frequency(q)[:, None], np.arange(256)[None, :], 256)
    c, s = np.cos(t), np.sin(t)
    full = np.stack([np.stack([c, s], 0), np.stack([-s, c], 0)], 0)
    full = full.reshape(2, 2, 16, 2, 16, 2, 8)
    return full.transpose(4, 5, 1, 6, 0, 3, 2).reshape(512, 64)


def first_twiddle():
    t = angle(np.arange(16)[:, None], np.arange(128)[None, :] % 16, 256)
    return np.concatenate([np.cos(t), np.sin(t)], 0).astype(np.float32)


def first_halves():
    t = angle(np.arange(2)[:, None], np.arange(16)[None, :], 16)
    c, s = np.cos(t), np.sin(t)
    full = np.stack([np.stack([c, -s], 1), np.stack([s, c], 1)], 1)
    return np.einsum("hsrx,ab->hsarbx", full, np.eye(8)).reshape(32, 256)


def first_inverse():
    p = np.arange(32)
    t = angle(frequency(p)[:, None], np.arange(256)[None, :], 256)
    full = np.stack([np.cos(t), np.sin(t)], 0).reshape(2, 16, 2, 256)
    return full.transpose(0, 2, 1, 3).reshape(64, 256)


def spans(sizes):
    return [(sum(sizes[:i]), size) for i, size in enumerate(sizes)]


def split(values):
    high = values.astype(BF16)
    low = (values - high.astype(F32)).astype(BF16)
    return high, low


def dot(a, b, dims=((1,), (0,))):
    return lax.dot_general(a, b, (dims, ((), ())), preferred_element_type=F32)


def dot3(a, b, dims=((1,), (0,))):
    return dot(a[0], b[0], dims) + (dot(a[0], b[1], dims) + dot(a[1], b[0], dims))


def lanes(shape):
    return lax.broadcasted_iota(jnp.int32, shape, len(shape) - 1)


def transpose_groups(blocks, width):
    blocks = list(blocks)
    count = len(blocks)
    group = lanes(blocks[0].shape) // width
    step = 1
    while step < count:
        upper = (group & step) != 0
        for i in range(count):
            if i & step:
                continue
            a, b = blocks[i], blocks[i | step]
            blocks[i] = jnp.where(upper, pltpu.roll(b, step * width, 1), a)
            blocks[i | step] = jnp.where(upper, b, pltpu.roll(a, 128 - step * width, 1))
        step *= 2
    return blocks


def fft(parts):
    count = len(parts)
    if count == 1:
        return parts
    even, odd = fft(parts[0::2]), fft(parts[1::2])
    out = [None] * count
    for j in range(count // 2):
        er, ei = even[j]
        orr, oi = odd[j]
        if j == 0:
            tr, ti = orr, oi
        elif 4 * j == count:
            tr, ti = oi, -orr
        else:
            c, s = math.cos(2 * math.pi * j / count), math.sin(2 * math.pi * j / count)
            tr, ti = orr * c + oi * s, oi * c - orr * s
        out[j] = (er + tr, ei + ti)
        out[j + count // 2] = (er - tr, ei - ti)
    return out


def slope(v):
    cumulative = 0.5 * (1.0 + lax.erf(v * (1.0 / math.sqrt(2.0))))
    density = jnp.exp(-0.5 * v * v) * (1.0 / math.sqrt(2.0 * math.pi))
    return cumulative + v * density


def start_kernel(x_hbm, pre_hbm, cot_hbm, table_ref, out_hbm, x, pre, cot, out, in_sems, out_sems):
    moves = []
    for i, (first, size) in enumerate(spans(START_PARTS)):
        at = pl.ds(first, size)
        three = [
            pltpu.make_async_copy(a.at[:, at], b.at[:, at], in_sems.at[n, i])
            for n, (a, b) in enumerate([(pre_hbm, pre), (cot_hbm, cot), (x_hbm, x)])
        ]
        for move in three:
            move.start()
        moves.append(three)
    both = table_ref[...]
    sends = []
    for i, (first, size) in enumerate(spans(START_PARTS)):
        for move in moves[i]:
            move.wait()
        own = slice(first, first + size)
        grad = cot[:, own] * slope(pre[:, own])
        for j in range(0, size, 2):
            rows = []
            for n in (j, j + 1):
                rows += [x[c, first + n] for c in range(4)] + [grad[c, n] for c in range(4)]
            rows = jnp.concatenate(rows, axis=0)
            for half in range(2):
                high, low = split(rows[:, 256 * half : 256 * half + 256])
                two = dot(both, high, ((1,), (1,)))
                done = two[:HALF] + (two[HALF:] + dot(both[:HALF], low, ((1,), (1,))))
                for n in range(2):
                    at = slice(HALF * half, HALF * half + HALF)
                    out[first + j + n, at] = done[:, 128 * n : 128 * n + 128]
        at = pl.ds(first, size)
        send = pltpu.make_async_copy(out.at[at], out_hbm.at[at], out_sems.at[i])
        send.start()
        sends.append(send)
    for send in sends:
        send.wait()


def second_kernel(in_ref, table_ref, real_ref, out_ref):
    for group in ((0,), (1, 2), (3, 4), (5, 6), (7,)):
        both = table_ref[...] if group[0] else real_ref[...]
        columns = []
        for k in group:
            at, size = (0, 8) if k == 0 else (16 * k - 8, 16)
            pieces = [(s, at + HALF * half) for s in range(16) for half in range(2)]
            columns.append(jnp.concatenate([in_ref[s, a : a + size, :] for s, a in pieces], axis=0))
        high, low = split(jnp.concatenate(columns, axis=1))
        two = dot(both, high)
        done = two[:64] + (two[64:] + dot(both[:64], low))
        for n, k in enumerate(group):
            for ri in range(2):
                for q in range(2):
                    rows = slice(32 * ri + 16 * q, 32 * ri + 16 * q + 16)
                    out_ref[pl.ds(ri * 16 + k * 2 + q, 16, stride=32), :] = done[
                        rows, 128 * n : 128 * n + 128
                    ]


def first_kernel(in_ref, tw_ref, table_ref, mix_ref, out_ref):
    parts = [(in_ref[32 * s : 32 * s + 16], in_ref[32 * s + 16 : 32 * s + 32]) for s in range(16)]
    rows = []
    for r, (re, im) in enumerate(fft(parts)):
        c, s = tw_ref[r : r + 1], tw_ref[16 + r : 17 + r]
        rows.append(jnp.concatenate([re * c + im * s, im * c - re * s], axis=1))
    data = split(jnp.concatenate(rows, axis=0))
    done = dot3((table_ref[:32], table_ref[32:]), data, ((1,), (1,)))
    lane = lanes((2, 128))
    for h in range(2):
        for t in range(2):
            tile = slice(128 * t, 128 * t + 128)
            blocks = [done[16 * h + 4 * g : 16 * h + 4 * g + 4, tile] for g in range(4)]
            for b, block in enumerate(transpose_groups(blocks, 32)):
                d = 8 * h + 4 * t + b
                out_ref[6 * d : 6 * d + 4] = block
                out_ref[6 * d + 4 : 6 * d + 6] = jnp.where(
                    lane < 64, mix_ref[4 * d : 4 * d + 2], mix_ref[4 * d + 2 : 4 * d + 4]
                )


def swap_halves(b1):
    turned = pltpu.roll(b1, 64, 1)
    return jnp.where(lanes(b1.shape) < 64, turned, -turned)


def mode_kernel(in_ref, w_ref, out_ref, fields_ref, b1_ref, mix_ref):
    fields = jnp.concatenate([in_ref[pl.ds(c, 16, stride=6), :] for c in range(4)], axis=0)
    fields_ref[...] = fields
    turned = jnp.concatenate([fields, fields], axis=0).T
    spread = jnp.where(lanes((32, 128)) < 64, turned[32:64], turned[96:])
    mode = lax.broadcasted_iota(jnp.int32, (32, 128), 0)
    b1 = spread * jnp.where((mode // 2) % 8 == 0, 1.0 / CELLS, 2.0 / CELLS)
    b2 = swap_halves(b1)
    lane = lanes((64, 128))
    total = jnp.zeros((64, 128), F32)
    for m in range(32):
        p, k, q = m // 16, (m // 2) % 8, m % 2
        at = ((p * 2 + q) * 8 + k) * 64
        weight = w_ref[at : at + 64]
        place = q + 4 * (k // 2) + 16 * p + 64 * (k % 2)
        real = jnp.sum(weight * b1[m : m + 1], axis=1, keepdims=True)
        imag = jnp.sum(weight * b2[m : m + 1], axis=1, keepdims=True)
        total = jnp.where(lane == place, real, total)
        total = jnp.where(lane == place + 2, imag, total)
    for c in range(2):
        two = total[32 * c : 32 * c + 16], total[32 * c + 16 : 32 * c + 32]
        out_ref[pl.ds(c, 16, stride=2), :] = two[0] + pltpu.roll(two[1], 32, 1)
    b1_ref[...] = b1
    mix = in_ref[4:6]
    for s in range(1, 16):
        mix = mix + in_ref[6 * s + 4 : 6 * s + 6]
    mix_ref[...] = mix


def outer_kernel(fields_ref, b1_ref, out_ref):
    fields, b1 = fields_ref[...], b1_ref[...]
    b2 = swap_halves(b1)
    for m in range(32):
        p, k, q = m // 16, (m // 2) % 8, m % 2
        at = ((p * 2 + q) * 8 + k) * 64
        real, imag = fields[:, m : m + 1], fields[:, 64 + m : 65 + m]
        out_ref[at : at + 64] = real * b1[m : m + 1] + imag * b2[m : m + 1]


def first_back_kernel(in_ref, t_ref, mix_ref, out_ref):
    parts = [in_ref[pl.ds(c // 2, 16, stride=2), :] for c in range(4)]
    lane = lanes((16, 128))
    rows = []
    for p in range(2):
        merged = None
        for c in range(4):
            shift = (16 * (c - p) - 32 * (c % 2)) % 128
            moved = pltpu.roll(parts[c], shift, 1) if shift else parts[c]
            merged = moved if merged is None else jnp.where((lane // 16) % 4 == c, moved, merged)
        rows.append(merged)
    re = jnp.concatenate(rows, axis=0)
    turned = jnp.where(
        (lanes((32, 128)) // 2) % 2 == 0, -pltpu.roll(re, 126, 1), pltpu.roll(re, 2, 1)
    )
    high, low = split(jnp.concatenate([re, turned], axis=0))
    done = dot(jnp.concatenate([high, high, low], axis=0), t_ref[...], ((0,), (0,)))
    mix = mix_ref[...]
    for t in range(2):
        blocks = [done[16 * b : 16 * b + 16, 128 * t : 128 * t + 128] for b in range(8)]
        for g, block in enumerate(transpose_groups(blocks, 16)):
            at = 18 * (8 * t + g)
            out_ref[at : at + 16] = block
            out_ref[at + 16 : at + 18] = mix


def second_back_kernel(in_ref, t_ref, out_ref):
    for k in range(4):
        rows = jnp.concatenate(
            [in_ref[pl.ds(4 * k + j, 16, stride=18), :] for j in range(4)], axis=0
        )
        high, low = split(rows)
        done = dot(t_ref[...], jnp.concatenate([high, high, low], axis=0))
        for y in range(16):
            for half in range(2):
                at, place = 32 * y + 16 * half, 64 * half + 16 * k
                out_ref[y, place : place + 16, :] = done[at : at + 16]
    mix = in_ref[16:18]
    for s in range(1, 16):
        mix = mix + in_ref[18 * s + 16 : 18 * s + 18]
    mix = jnp.concatenate([mix, pltpu.roll(mix, 64, 1)], axis=0)
    for y in range(16):
        out_ref[y, 8:12, 0:64] = mix[:, :64]


def end_kernel(in_ref, direct_ref, table_ref, out_hbm, mix_hbm, out, mix, mix_sem, out_sems):
    for d in range(16):
        mix[4 * d : 4 * d + 4] = in_ref[d, 8:12, 0:64] * (1.0 / math.sqrt(CELLS))
    mix_move = pltpu.make_async_copy(mix, mix_hbm, mix_sem)
    mix_move.start()
    sends = []
    for i, (first, size) in enumerate(spans(END_PARTS)):
        rows = [[], []]
        for j in range(size):
            turned = in_ref[first + j].T
            for half in range(2):
                at = slice(64 * half, 64 * half + 64)
                rows[half].append(jnp.concatenate([turned[:64, at], turned[64:, at]], axis=1))
        parts = []
        for half in range(2):
            high, low = split(jnp.concatenate(rows[half], axis=0))
            parts.append(
                dot(jnp.concatenate([high, high], axis=1), table_ref[...]) + dot(low, table_ref[:128])
            )
        done = jnp.concatenate(parts, axis=1)
        for j in range(size):
            for c in range(4):
                at = 64 * j + 16 * c
                out[c, first + j] = direct_ref[c, first + j] + done[at : at + 16]
        at = pl.ds(first, size)
        send = pltpu.make_async_copy(out.at[:, at], out_hbm.at[:, at], out_sems.at[i])
        send.start()
        sends.append(send)
    for send in sends:
        send.wait()
    mix_move.wait()


def side_kernel(x_ref, pre_ref, cot_ref, weight_ref, direct_ref, mix_ref):
    high, low = split(weight_ref[...])
    weight = jnp.concatenate([high, low, high], axis=1)
    total = jnp.zeros((64, 64), F32)
    for x in range(16):
        field = split(x_ref[pl.ds(x, 64, stride=16), :])
        at = pl.ds(x, 64, stride=16)
        gh, gl = split(cot_ref[at, :] * slope(pre_ref[at, :]))
        total = total + dot3(field, (gh, gl), ((1,), (1,)))
        direct_ref[pl.ds(x, 64, stride=16), :] = dot(weight, jnp.concatenate([gh, gh, gl], axis=0))
    total = jnp.concatenate([total, total], axis=1)
    first = pl.program_id(0) == 0

    @pl.when(first)
    def _():
        mix_ref[...] = total

    @pl.when(jnp.logical_not(first))
    def _():
        mix_ref[...] += total


def params(mebibytes):
    return pltpu.CompilerParams(vmem_limit_bytes=mebibytes << 20)


def whole(count):
    return [pl.BlockSpec(memory_space=pltpu.VMEM)] * count


def struct(*shape):
    return jax.ShapeDtypeStruct(shape, F32)


def call(body, outs, args, mebibytes=12, cost=None):
    many = isinstance(outs, tuple)
    return pl.pallas_call(
        body,
        out_shape=outs,
        in_specs=whole(len(args)),
        out_specs=tuple(whole(len(outs))) if many else whole(1)[0],
        compiler_params=params(mebibytes),
        cost_estimate=cost,
    )(*args)


def exchange(values, axis):
    return lax.all_to_all(values, axis, split_axis=0, concat_axis=0, tiled=True)


def stacked(table):
    high, low = pair(table)
    return np.concatenate([high, low, high], axis=1)


def per_device(inputs, pre_act, cotangent, mix_weight, spectral_weight):
    anywhere = pl.BlockSpec(memory_space=pltpu.HBM)
    field = pltpu.VMEM((4, N, N, 512), F32)
    shaped = [a.reshape(4, N, N, 512) for a in (inputs, pre_act, cotangent)]
    depth = pl.pallas_call(
        start_kernel,
        out_shape=struct(N, ROWS, 128),
        in_specs=[anywhere] * 3 + whole(1),
        out_specs=anywhere,
        scratch_shapes=[
            field,
            field,
            field,
            pltpu.VMEM((N, ROWS, 128), F32),
            pltpu.SemaphoreType.DMA((3, len(START_PARTS))),
            pltpu.SemaphoreType.DMA((len(START_PARTS),)),
        ],
        compiler_params=params(60),
    )(*shaped, column(depth_sent()))

    tile_spec = pl.BlockSpec((1024, 128), lambda i: (0, i))
    direct, mix = pl.pallas_call(
        side_kernel,
        grid=(4,),
        out_shape=(struct(1024, 512), struct(64, 128)),
        in_specs=[tile_spec] * 3 + [pl.BlockSpec((64, 64), lambda i: (0, 0))],
        out_specs=(tile_spec, pl.BlockSpec((64, 128), lambda i: (0, 0))),
        compiler_params=params(60),
        cost_estimate=pl.CostEstimate(flops=1 << 30, bytes_accessed=6 << 20, transcendentals=0),
    )(*[a.reshape(1024, 512) for a in (inputs, pre_act, cotangent)], mix_weight)
    depth, direct, mix = lax.optimization_barrier((exchange(depth, "py"), direct, mix))
    along_second = call(
        second_kernel, struct(512, 128), (depth, column(second_forward()), column(second_real()))
    )
    along_second = exchange(along_second.reshape(16, 32, 128), "px").reshape(512, 128)
    along_first = call(
        first_kernel,
        struct(96, 128),
        (along_second, jnp.asarray(first_twiddle()), column(first_halves()), mix),
    )
    spectra = exchange(along_first.reshape(16, 1, 768), "py").reshape(96, 128)
    mode_back, fields, b1, mix = call(
        mode_kernel,
        (struct(32, 128), struct(64, 128), struct(32, 128), struct(2, 128)),
        (spectra, spectral_weight.reshape(2048, 128)),
    )
    mode_back = exchange(mode_back.reshape(16, 2, 128), "py").reshape(32, 128)
    spectral_grad = call(
        outer_kernel,
        struct(2048, 128),
        (fields, b1),
        8,
        pl.CostEstimate(flops=1 << 20, bytes_accessed=1 << 20, transcendentals=0),
    ).reshape(spectral_weight.shape)
    first_high, first_low = pair(first_inverse())
    first_table = np.concatenate([first_high, first_low, first_high], axis=0)
    first_back = call(
        first_back_kernel, struct(288, 128), (mode_back, jnp.asarray(first_table), mix)
    )
    first_back = exchange(first_back.reshape(16, 1, 2304), "px").reshape(288, 128)
    first_back, spectral_grad = lax.optimization_barrier((first_back, spectral_grad))
    second_back = call(
        second_back_kernel,
        struct(16, 128, 128),
        (first_back, jnp.asarray(stacked(second_inverse()))),
    )
    gathered = exchange(second_back, "py")
    input_grad, mix_grad = pl.pallas_call(
        end_kernel,
        out_shape=(struct(4, N, N, 512), struct(C, C)),
        in_specs=whole(3),
        out_specs=(anywhere, anywhere),
        scratch_shapes=[
            field,
            pltpu.VMEM((C, C), F32),
            pltpu.SemaphoreType.DMA,
            pltpu.SemaphoreType.DMA((len(END_PARTS),)),
        ],
        compiler_params=params(20),
    )(gathered, direct.reshape(4, N, N, 512), column(depth_inverse()))
    return (input_grad.reshape(inputs.shape), spectral_grad, mix_grad)


def solution(mesh):
    placed = (
        P(None, "px", "py"),
        P(None, "px", "py"),
        P(None, "px", "py"),
        P(),
        P("py", "px", None, None, None),
    )
    return jax.shard_map(
        per_device,
        mesh=mesh,
        in_specs=placed,
        out_specs=(P(None, "px", "py"), P("py", "px", None, None, None), P()),
        check_vma=False,
    )
```

```python
import math

import jax
import jax.numpy as jnp
import ml_dtypes
import numpy as np
from jax import lax
from jax.experimental import pallas as pl
from jax.experimental.pallas import tpu as pltpu
from jax.sharding import PartitionSpec as P

C = 64
NX = 256
NY = 256
NZ = 32
MZ = 8
CELLS = NX * NY * NZ
N = 16
ROWS = 240
HALF = ROWS // 2
START_PARTS = (4, 4, 4, 4)
END_PARTS = (4, 4, 4, 4)
F32 = jnp.float32
BF16 = jnp.bfloat16


def pair(table):
    high = table.astype(ml_dtypes.bfloat16)
    low = (table - high.astype(np.float64)).astype(high.dtype)
    return high, low


def column(table):
    return jnp.asarray(np.concatenate(pair(table), axis=0))


def frequency(index):
    return np.where(index < 16, index, index - 32)


def angle(a, b, length):
    return 2.0 * np.pi / length * np.mod(a * b, length)


def depth_parts(cells):
    k, z = np.arange(8)[:, None], np.arange(32)[None, :]
    t = angle(k, z, 32)
    parts = np.stack([np.cos(t), -np.sin(t)], 1)
    return np.einsum("krz,ab->krabz", parts, np.eye(cells)).reshape(8, 2, cells, cells * 32)


def depth_sent():
    return np.delete(depth_parts(8).reshape(128, 256), np.arange(8, 16), axis=0)


def depth_inverse():
    return depth_parts(8).reshape(4, 2, 16, 256).transpose(1, 0, 2, 3).reshape(128, 256)


def second_forward():
    q = np.arange(32)
    t = angle(frequency(q)[:, None], np.arange(256)[None, :], 256)
    c, s = np.cos(t), np.sin(t)
    full = np.stack([np.stack([c, s], 1), np.stack([-s, c], 1)], 0)
    full = full.reshape(2, 16, 2, 2, 16, 2, 8)
    return full.transpose(0, 2, 1, 4, 5, 3, 6).reshape(64, 512)


def second_real():
    return second_forward().reshape(64, 32, 2, 8)[:, :, 0].reshape(64, 256)


def second_inverse():
    q = np.arange(32)
    t = angle(frequency(q)[:, None], np.arange(256)[None, :], 256)
    c, s = np.cos(t), np.sin(t)
    full = np.stack([np.stack([c, s], 0), np.stack([-s, c], 0)], 0)
    full = full.reshape(2, 2, 16, 2, 16, 2, 8)
    return full.transpose(4, 5, 1, 6, 0, 3, 2).reshape(512, 64)


def first_twiddle():
    t = angle(np.arange(16)[:, None], np.arange(128)[None, :] % 16, 256)
    return np.concatenate([np.cos(t), np.sin(t)], 0).astype(np.float32)


def first_halves():
    t = angle(np.arange(2)[:, None], np.arange(16)[None, :], 16)
    c, s = np.cos(t), np.sin(t)
    full = np.stack([np.stack([c, -s], 1), np.stack([s, c], 1)], 1)
    return np.einsum("hsrx,ab->hsarbx", full, np.eye(8)).reshape(32, 256)


def first_inverse():
    p = np.arange(32)
    t = angle(frequency(p)[:, None], np.arange(256)[None, :], 256)
    full = np.stack([np.cos(t), np.sin(t)], 0).reshape(2, 16, 2, 256)
    return full.transpose(0, 2, 1, 3).reshape(64, 256)


def spans(sizes):
    return [(sum(sizes[:i]), size) for i, size in enumerate(sizes)]


def split(values):
    high = values.astype(BF16)
    low = (values - high.astype(F32)).astype(BF16)
    return high, low


def dot(a, b, dims=((1,), (0,))):
    return lax.dot_general(a, b, (dims, ((), ())), preferred_element_type=F32)


def dot3(a, b, dims=((1,), (0,))):
    return dot(a[0], b[0], dims) + (dot(a[0], b[1], dims) + dot(a[1], b[0], dims))


def lanes(shape):
    return lax.broadcasted_iota(jnp.int32, shape, len(shape) - 1)


def transpose_groups(blocks, width):
    blocks = list(blocks)
    count = len(blocks)
    group = lanes(blocks[0].shape) // width
    step = 1
    while step < count:
        upper = (group & step) != 0
        for i in range(count):
            if i & step:
                continue
            a, b = blocks[i], blocks[i | step]
            blocks[i] = jnp.where(upper, pltpu.roll(b, step * width, 1), a)
            blocks[i | step] = jnp.where(upper, b, pltpu.roll(a, 128 - step * width, 1))
        step *= 2
    return blocks


def fft(parts):
    count = len(parts)
    if count == 1:
        return parts
    even, odd = fft(parts[0::2]), fft(parts[1::2])
    out = [None] * count
    for j in range(count // 2):
        er, ei = even[j]
        orr, oi = odd[j]
        if j == 0:
            tr, ti = orr, oi
        elif 4 * j == count:
            tr, ti = oi, -orr
        else:
            c, s = math.cos(2 * math.pi * j / count), math.sin(2 * math.pi * j / count)
            tr, ti = orr * c + oi * s, oi * c - orr * s
        out[j] = (er + tr, ei + ti)
        out[j + count // 2] = (er - tr, ei - ti)
    return out


def slope(v):
    cumulative = 0.5 * (1.0 + lax.erf(v * (1.0 / math.sqrt(2.0))))
    density = jnp.exp(-0.5 * v * v) * (1.0 / math.sqrt(2.0 * math.pi))
    return cumulative + v * density


def start_kernel(x_hbm, pre_hbm, cot_hbm, table_ref, out_hbm, x, pre, cot, out, in_sems, out_sems):
    moves = []
    for i, (first, size) in enumerate(spans(START_PARTS)):
        at = pl.ds(first, size)
        three = [
            pltpu.make_async_copy(a.at[:, at], b.at[:, at], in_sems.at[n, i])
            for n, (a, b) in enumerate([(pre_hbm, pre), (cot_hbm, cot), (x_hbm, x)])
        ]
        for move in three:
            move.start()
        moves.append(three)
    both = table_ref[...]
    sends = []
    for i, (first, size) in enumerate(spans(START_PARTS)):
        for move in moves[i]:
            move.wait()
        own = slice(first, first + size)
        grad = cot[:, own] * slope(pre[:, own])
        for j in range(0, size, 2):
            rows = []
            for n in (j, j + 1):
                rows += [x[c, first + n] for c in range(4)] + [grad[c, n] for c in range(4)]
            rows = jnp.concatenate(rows, axis=0)
            for half in range(2):
                high, low = split(rows[:, 256 * half : 256 * half + 256])
                two = dot(both, high, ((1,), (1,)))
                done = two[:128] + (two[128:] + dot(both[:128], low, ((1,), (1,))))
                for n in range(2):
                    at = slice(HALF * half, HALF * half + HALF)
                    out[first + j + n, at] = done[:HALF, 128 * n : 128 * n + 128]
        at = pl.ds(first, size)
        send = pltpu.make_async_copy(out.at[at], out_hbm.at[at], out_sems.at[i])
        send.start()
        sends.append(send)
    for send in sends:
        send.wait()


def second_kernel(in_ref, table_ref, real_ref, out_ref):
    for group in ((0,), (1, 2), (3, 4), (5, 6), (7,)):
        both = table_ref[...] if group[0] else real_ref[...]
        columns = []
        for k in group:
            at, size = (0, 8) if k == 0 else (16 * k - 8, 16)
            pieces = [(s, at + HALF * half) for s in range(16) for half in range(2)]
            columns.append(jnp.concatenate([in_ref[s, a : a + size, :] for s, a in pieces], axis=0))
        high, low = split(jnp.concatenate(columns, axis=1))
        two = dot(both, high)
        done = two[:64] + (two[64:] + dot(both[:64], low))
        for n, k in enumerate(group):
            for ri in range(2):
                for q in range(2):
                    rows = slice(32 * ri + 16 * q, 32 * ri + 16 * q + 16)
                    out_ref[pl.ds(ri * 16 + k * 2 + q, 16, stride=32), :] = done[
                        rows, 128 * n : 128 * n + 128
                    ]


def first_kernel(in_ref, tw_ref, table_ref, mix_ref, out_ref):
    parts = [(in_ref[32 * s : 32 * s + 16], in_ref[32 * s + 16 : 32 * s + 32]) for s in range(16)]
    rows = []
    for r, (re, im) in enumerate(fft(parts)):
        c, s = tw_ref[r : r + 1], tw_ref[16 + r : 17 + r]
        rows.append(jnp.concatenate([re * c + im * s, im * c - re * s], axis=1))
    data = split(jnp.concatenate(rows, axis=0))
    done = dot3((table_ref[:32], table_ref[32:]), data, ((1,), (1,)))
    lane = lanes((2, 128))
    for h in range(2):
        for t in range(2):
            tile = slice(128 * t, 128 * t + 128)
            blocks = [done[16 * h + 4 * g : 16 * h + 4 * g + 4, tile] for g in range(4)]
            for b, block in enumerate(transpose_groups(blocks, 32)):
                d = 8 * h + 4 * t + b
                out_ref[6 * d : 6 * d + 4] = block
                out_ref[6 * d + 4 : 6 * d + 6] = jnp.where(
                    lane < 64, mix_ref[4 * d : 4 * d + 2], mix_ref[4 * d + 2 : 4 * d + 4]
                )


def swap_halves(b1):
    turned = pltpu.roll(b1, 64, 1)
    return jnp.where(lanes(b1.shape) < 64, turned, -turned)


def mode_kernel(in_ref, w_ref, out_ref, fields_ref, b1_ref, mix_ref):
    fields = jnp.concatenate([in_ref[pl.ds(c, 16, stride=6), :] for c in range(4)], axis=0)
    fields_ref[...] = fields
    turned = jnp.concatenate([fields, fields], axis=0).T
    spread = jnp.where(lanes((32, 128)) < 64, turned[32:64], turned[96:])
    mode = lax.broadcasted_iota(jnp.int32, (32, 128), 0)
    b1 = spread * jnp.where((mode // 2) % 8 == 0, 1.0 / CELLS, 2.0 / CELLS)
    b2 = swap_halves(b1)
    lane = lanes((64, 128))
    total = jnp.zeros((64, 128), F32)
    for m in range(32):
        p, k, q = m // 16, (m // 2) % 8, m % 2
        at = ((p * 2 + q) * 8 + k) * 64
        weight = w_ref[at : at + 64]
        place = q + 4 * (k // 2) + 16 * p + 64 * (k % 2)
        real = jnp.sum(weight * b1[m : m + 1], axis=1, keepdims=True)
        imag = jnp.sum(weight * b2[m : m + 1], axis=1, keepdims=True)
        total = jnp.where(lane == place, real, total)
        total = jnp.where(lane == place + 2, imag, total)
    for c in range(2):
        two = total[32 * c : 32 * c + 16], total[32 * c + 16 : 32 * c + 32]
        out_ref[pl.ds(c, 16, stride=2), :] = two[0] + pltpu.roll(two[1], 32, 1)
    b1_ref[...] = b1
    mix = in_ref[4:6]
    for s in range(1, 16):
        mix = mix + in_ref[6 * s + 4 : 6 * s + 6]
    mix_ref[...] = mix


def outer_kernel(fields_ref, b1_ref, out_ref):
    fields, b1 = fields_ref[...], b1_ref[...]
    b2 = swap_halves(b1)
    for m in range(32):
        p, k, q = m // 16, (m // 2) % 8, m % 2
        at = ((p * 2 + q) * 8 + k) * 64
        real, imag = fields[:, m : m + 1], fields[:, 64 + m : 65 + m]
        out_ref[at : at + 64] = real * b1[m : m + 1] + imag * b2[m : m + 1]


def first_back_kernel(in_ref, t_ref, mix_ref, out_ref):
    parts = [in_ref[pl.ds(c // 2, 16, stride=2), :] for c in range(4)]
    lane = lanes((16, 128))
    rows = []
    for p in range(2):
        merged = None
        for c in range(4):
            shift = (16 * (c - p) - 32 * (c % 2)) % 128
            moved = pltpu.roll(parts[c], shift, 1) if shift else parts[c]
            merged = moved if merged is None else jnp.where((lane // 16) % 4 == c, moved, merged)
        rows.append(merged)
    re = jnp.concatenate(rows, axis=0)
    turned = jnp.where(
        (lanes((32, 128)) // 2) % 2 == 0, -pltpu.roll(re, 126, 1), pltpu.roll(re, 2, 1)
    )
    high, low = split(jnp.concatenate([re, turned], axis=0))
    done = dot(jnp.concatenate([high, high, low], axis=0), t_ref[...], ((0,), (0,)))
    mix = mix_ref[...]
    for t in range(2):
        blocks = [done[16 * b : 16 * b + 16, 128 * t : 128 * t + 128] for b in range(8)]
        for g, block in enumerate(transpose_groups(blocks, 16)):
            at = 18 * (8 * t + g)
            out_ref[at : at + 16] = block
            out_ref[at + 16 : at + 18] = mix


def second_back_kernel(in_ref, t_ref, out_ref):
    for k in range(4):
        rows = jnp.concatenate(
            [in_ref[pl.ds(4 * k + j, 16, stride=18), :] for j in range(4)], axis=0
        )
        high, low = split(rows)
        done = dot(t_ref[...], jnp.concatenate([high, high, low], axis=0))
        for y in range(16):
            for half in range(2):
                at, place = 32 * y + 16 * half, 64 * half + 16 * k
                out_ref[y, place : place + 16, :] = done[at : at + 16]
    mix = in_ref[16:18]
    for s in range(1, 16):
        mix = mix + in_ref[18 * s + 16 : 18 * s + 18]
    mix = jnp.concatenate([mix, pltpu.roll(mix, 64, 1)], axis=0)
    for y in range(16):
        out_ref[y, 8:12, 0:64] = mix[:, :64]


def end_kernel(in_ref, direct_ref, table_ref, out_hbm, mix_hbm, out, mix, mix_sem, out_sems):
    for d in range(16):
        mix[4 * d : 4 * d + 4] = in_ref[d, 8:12, 0:64] * (1.0 / math.sqrt(CELLS))
    mix_move = pltpu.make_async_copy(mix, mix_hbm, mix_sem)
    mix_move.start()
    sends = []
    for i, (first, size) in enumerate(spans(END_PARTS)):
        rows = [[], []]
        for j in range(size):
            turned = in_ref[first + j].T
            for half in range(2):
                at = slice(64 * half, 64 * half + 64)
                rows[half].append(jnp.concatenate([turned[:64, at], turned[64:, at]], axis=1))
        parts = []
        for half in range(2):
            high, low = split(jnp.concatenate(rows[half], axis=0))
            parts.append(
                dot(jnp.concatenate([high, high], axis=1), table_ref[...]) + dot(low, table_ref[:128])
            )
        done = jnp.concatenate(parts, axis=1)
        for j in range(size):
            for c in range(4):
                at = 64 * j + 16 * c
                out[c, first + j] = direct_ref[c, first + j] + done[at : at + 16]
        at = pl.ds(first, size)
        send = pltpu.make_async_copy(out.at[:, at], out_hbm.at[:, at], out_sems.at[i])
        send.start()
        sends.append(send)
    for send in sends:
        send.wait()
    mix_move.wait()


def side_kernel(x_ref, pre_ref, cot_ref, weight_ref, direct_ref, mix_ref):
    high, low = split(weight_ref[...])
    weight = jnp.concatenate([high, low, high], axis=1)
    total = jnp.zeros((64, 64), F32)
    for x in range(16):
        field = split(x_ref[pl.ds(x, 64, stride=16), :])
        at = pl.ds(x, 64, stride=16)
        gh, gl = split(cot_ref[at, :] * slope(pre_ref[at, :]))
        total = total + dot3(field, (gh, gl), ((1,), (1,)))
        direct_ref[pl.ds(x, 64, stride=16), :] = dot(weight, jnp.concatenate([gh, gh, gl], axis=0))
    total = jnp.concatenate([total, total], axis=1)
    first = pl.program_id(0) == 0

    @pl.when(first)
    def _():
        mix_ref[...] = total

    @pl.when(jnp.logical_not(first))
    def _():
        mix_ref[...] += total


def params(mebibytes):
    return pltpu.CompilerParams(vmem_limit_bytes=mebibytes << 20)


def whole(count):
    return [pl.BlockSpec(memory_space=pltpu.VMEM)] * count


def struct(*shape):
    return jax.ShapeDtypeStruct(shape, F32)


def call(body, outs, args, mebibytes=12, cost=None):
    many = isinstance(outs, tuple)
    return pl.pallas_call(
        body,
        out_shape=outs,
        in_specs=whole(len(args)),
        out_specs=tuple(whole(len(outs))) if many else whole(1)[0],
        compiler_params=params(mebibytes),
        cost_estimate=cost,
    )(*args)


def exchange(values, axis):
    return lax.all_to_all(values, axis, split_axis=0, concat_axis=0, tiled=True)


def stacked(table):
    high, low = pair(table)
    return np.concatenate([high, low, high], axis=1)


def per_device(inputs, pre_act, cotangent, mix_weight, spectral_weight):
    anywhere = pl.BlockSpec(memory_space=pltpu.HBM)
    field = pltpu.VMEM((4, N, N, 512), F32)
    shaped = [a.reshape(4, N, N, 512) for a in (inputs, pre_act, cotangent)]
    depth = pl.pallas_call(
        start_kernel,
        out_shape=struct(N, ROWS, 128),
        in_specs=[anywhere] * 3 + whole(1),
        out_specs=anywhere,
        scratch_shapes=[
            field,
            field,
            field,
            pltpu.VMEM((N, ROWS, 128), F32),
            pltpu.SemaphoreType.DMA((3, len(START_PARTS))),
            pltpu.SemaphoreType.DMA((len(START_PARTS),)),
        ],
        compiler_params=params(60),
    )(*shaped, column(np.pad(depth_sent(), ((0, 128 - HALF), (0, 0)))))

    tile_spec = pl.BlockSpec((1024, 128), lambda i: (0, i))
    direct, mix = pl.pallas_call(
        side_kernel,
        grid=(4,),
        out_shape=(struct(1024, 512), struct(64, 128)),
        in_specs=[tile_spec] * 3 + [pl.BlockSpec((64, 64), lambda i: (0, 0))],
        out_specs=(tile_spec, pl.BlockSpec((64, 128), lambda i: (0, 0))),
        compiler_params=params(60),
        cost_estimate=pl.CostEstimate(flops=1 << 30, bytes_accessed=6 << 20, transcendentals=0),
    )(*[a.reshape(1024, 512) for a in (inputs, pre_act, cotangent)], mix_weight)
    depth, direct, mix = lax.optimization_barrier((exchange(depth, "py"), direct, mix))
    along_second = call(
        second_kernel, struct(512, 128), (depth, column(second_forward()), column(second_real()))
    )
    along_second = exchange(along_second.reshape(16, 32, 128), "px").reshape(512, 128)
    along_first = call(
        first_kernel,
        struct(96, 128),
        (along_second, jnp.asarray(first_twiddle()), column(first_halves()), mix),
    )
    spectra = exchange(along_first.reshape(16, 1, 768), "py").reshape(96, 128)
    mode_back, fields, b1, mix = call(
        mode_kernel,
        (struct(32, 128), struct(64, 128), struct(32, 128), struct(2, 128)),
        (spectra, spectral_weight.reshape(2048, 128)),
    )
    mode_back = exchange(mode_back.reshape(16, 2, 128), "py").reshape(32, 128)
    spectral_grad = call(
        outer_kernel,
        struct(2048, 128),
        (fields, b1),
        8,
        pl.CostEstimate(flops=1 << 20, bytes_accessed=1 << 20, transcendentals=0),
    ).reshape(spectral_weight.shape)
    first_high, first_low = pair(first_inverse())
    first_table = np.concatenate([first_high, first_low, first_high], axis=0)
    first_back = call(
        first_back_kernel, struct(288, 128), (mode_back, jnp.asarray(first_table), mix)
    )
    first_back = exchange(first_back.reshape(16, 1, 2304), "px").reshape(288, 128)
    first_back, spectral_grad = lax.optimization_barrier((first_back, spectral_grad))
    second_back = call(
        second_back_kernel,
        struct(16, 128, 128),
        (first_back, jnp.asarray(stacked(second_inverse()))),
    )
    gathered = exchange(second_back, "py")
    input_grad, mix_grad = pl.pallas_call(
        end_kernel,
        out_shape=(struct(4, N, N, 512), struct(C, C)),
        in_specs=whole(3),
        out_specs=(anywhere, anywhere),
        scratch_shapes=[
            field,
            pltpu.VMEM((C, C), F32),
            pltpu.SemaphoreType.DMA,
            pltpu.SemaphoreType.DMA((len(END_PARTS),)),
        ],
        compiler_params=params(20),
    )(gathered, direct.reshape(4, N, N, 512), column(depth_inverse()))
    return (input_grad.reshape(inputs.shape), spectral_grad, mix_grad)


def solution(mesh):
    placed = (
        P(None, "px", "py"),
        P(None, "px", "py"),
        P(None, "px", "py"),
        P(),
        P("py", "px", None, None, None),
    )
    return jax.shard_map(
        per_device,
        mesh=mesh,
        in_specs=placed,
        out_specs=(P(None, "px", "py"), P("py", "px", None, None, None), P()),
        check_vma=False,
    )
```
